256 devices in a mesh: dp: 32 (over y, z_hi, core), tensor: 8 (over x, z_lo).
Axes of the slice: x: 4, y: 4, z: 8 (z_hi: 4, z_lo: 2; z = z_hi * 2 + z_lo), core: 2. Of those that a mesh axis runs over, the one named last changes fastest.
Arguments:
- student_hidden: bfloat16 [32768, 3584], P(('dp', 'tensor')), may hold values from -140 to 140
- norm_gain: float32 [3584], replicated, may hold values from 0.1 to 1.9
- projection: bfloat16 [3584, 4096], P('dp', 'tensor'), may hold values from -0.09375 to 0.09375
- teacher_terms: bfloat16 [8, 32768, 4096], P('tensor', 'dp'), may hold values from -80 to 80
Outputs:
- distill_loss: float32 [], replicated
- hidden_grad: bfloat16 [32768, 3584], P(('dp', 'tensor'))
- projection_update: float32 [3584, 4096], P('dp', 'tensor')
- gain_update: float32 [3584], replicated
The draws below stay inside these ranges and needn't reach their ends.
All inputs are finite; a program needn't handle non-finite values.
Results may differ from the reference program's by a relative error of at most 0.028.
Values may be sent and summed in bfloat16 or wider, within the bound.
A program may use at most 64 MiB of HBM per device.

```python
import math
import jax
import jax.numpy as jnp
from jax import lax

DS = 3584
DT = 4096
TOKENS = 32768
N_DP = 32
N_TENSOR = 8


def draw_student_hidden(key, part):
    key = jax.random.fold_in(key, 5)
    key_base, key_scale, key_rows = jax.random.split(key, 3)
    position = jnp.arange(DS, dtype=jnp.float32) / DS
    row_scale = jnp.exp(jax.random.uniform(key_rows, (TOKENS, 1), jnp.float32, math.log(0.5), math.log(2.0)))
    jitter = jax.random.uniform(key_scale, (DS,), jnp.float32, 0.7, 1.4)
    noise_base = jnp.clip(jax.random.normal(key_base, (TOKENS, DS), jnp.float32), -5.0, 5.0)
    values = noise_base * 10.0 ** position * jitter * row_scale
    return values.astype(jnp.bfloat16)


def draw_teacher_terms(key, part):
    key = jax.random.fold_in(key, 9)
    key_scale, key_noise = jax.random.split(key, 2)
    position = jnp.arange(DT, dtype=jnp.float32) / DT
    row_place = jnp.arange(TOKENS, dtype=jnp.float32) / TOKENS
    jitter = jax.random.uniform(key_scale, (DT,), jnp.float32, 0.7, 1.4)
    part_keys = jax.random.split(key_noise, N_TENSOR)
    spread = 1.0 / math.sqrt(N_TENSOR)
    col_scale = 0.5 * 10.0 ** position * jitter
    row_scale = 3.0 ** row_place

    def draw_part(part_key):
        noise = jnp.clip(jax.random.normal(part_key, (TOKENS, DT), jnp.float32), -5.0, 5.0)
        return (noise * row_scale[:, None] * col_scale * spread).astype(jnp.bfloat16)
    return lax.map(draw_part, part_keys)


def block_levels(key, dims, pieces, smallest, top_value):
    def one(axis_at, blocks):
        draws = jax.random.uniform(jax.random.fold_in(jax.random.fold_in(key, 6), axis_at), (blocks,), jnp.float32, smallest / len(pieces), top_value / len(pieces))
        return jnp.repeat(jnp.exp(draws), dims[axis_at] // blocks).reshape((-1,) + (1,) * (len(dims) - axis_at - 1))

    loudness = one(*pieces[0])
    for cut in pieces[1:]:
        loudness = loudness * one(*cut)
    return loudness


def bell_draw(stream_key, shape, scale, limit, shards=(), held_as=jnp.bfloat16):
    factor_of = block_levels(stream_key, shape, shards, -0.22, 0.18) if shards else 1.0
    array = jax.random.normal(stream_key, shape, jnp.float32) * scale * factor_of
    return jnp.minimum(jnp.maximum(array, -limit), limit).astype(held_as)


def setup_inputs(seed: int = 0) -> dict:
    splits = jax.random.split(jax.random.key(seed), 5)
    return {
        "student_hidden": draw_student_hidden(jax.random.fold_in(splits[4], 71), 0),
        "norm_gain": jnp.clip(1.0 + 0.18 * jax.random.normal(splits[1], (DS,), jnp.float32), 0.1, 1.9),
        "projection": bell_draw(splits[2], (DS, DT), DS ** -0.5, 0.09375, ((0, 32), (1, 8))),
        "teacher_terms": draw_teacher_terms(jax.random.fold_in(splits[4], 71), 0),
    }


epsilon = 1e-06

def reference(student_hidden, norm_gain, projection, teacher_terms):
    block_rows = TOKENS // N_DP
    col_width = DT // N_TENSOR
    proj_wide = projection.astype(jnp.float32)

    def one_block(totals, block_index):
        grad_sum, gain_sum, loss_sum = totals
        offset = block_index * block_rows
        hidden = lax.dynamic_slice_in_dim(student_hidden, offset, block_rows, 0).astype(jnp.float32)
        inv_rms = lax.rsqrt(lax.optimization_barrier(jnp.mean(hidden * hidden, axis=1, keepdims=True)) + epsilon)
        scaled = hidden * inv_rms
        normed = (scaled * norm_gain).astype(jnp.bfloat16)
        predicted = jnp.dot(normed, projection, preferred_element_type=jnp.float32).astype(jnp.bfloat16)
        teacher_part = lax.dynamic_slice_in_dim(teacher_terms, offset, block_rows, 1).astype(jnp.float32)
        target = lax.optimization_barrier(jnp.sum(teacher_part, axis=0))
        mismatch = predicted.astype(jnp.float32) - target
        loss_sum = loss_sum + jnp.sum(mismatch * mismatch)
        pred_grad = mismatch.astype(jnp.bfloat16)
        block_terms = jnp.einsum('rkc,dkc->krd', pred_grad.astype(jnp.float32).reshape(block_rows, N_TENSOR, col_width), proj_wide.reshape(DS, N_TENSOR, col_width))
        normed_grad = lax.optimization_barrier(jnp.sum(lax.optimization_barrier(block_terms.astype(jnp.bfloat16)).astype(jnp.float32), axis=0))
        weight_term = lax.dot_general(normed, pred_grad, (((0,), (0,)), ((), ())), preferred_element_type=jnp.float32)
        grad_sum = grad_sum + lax.optimization_barrier(weight_term.astype(jnp.bfloat16)).astype(jnp.float32)
        gain_sum = gain_sum + lax.optimization_barrier(jnp.sum(normed_grad * scaled, axis=0))
        gain_scaled = normed_grad * norm_gain
        hidden_grad = (inv_rms * (gain_scaled - scaled * lax.optimization_barrier(jnp.mean(gain_scaled * scaled, axis=1, keepdims=True)))).astype(jnp.bfloat16)
        return ((grad_sum, gain_sum, loss_sum), hidden_grad)
    start_totals = (jnp.zeros((DS, DT), jnp.float32), jnp.zeros((DS,), jnp.float32), jnp.zeros((), jnp.float32))
    totals, grads = lax.scan(one_block, start_totals, jnp.arange(N_DP, dtype=jnp.int32))
    grad_sum, gain_sum, loss_sum = totals
    distill_loss = loss_sum / (TOKENS * DT)
    squares = jnp.sum(grad_sum * grad_sum) + jnp.sum(gain_sum * gain_sum)
    factor = lax.rsqrt(squares / (DS * DT + DS) + epsilon)
    return (distill_loss, grads.reshape(TOKENS, DS), grad_sum * factor, gain_sum * factor)
```

```python
import jax
import jax.numpy as jnp
from jax import lax
from jax.experimental import pallas as pl
from jax.experimental.pallas import tpu as pltpu
from jax.sharding import PartitionSpec as P

epsilon = 1e-06
MESH = pl.DeviceIdType.MESH
F32 = jnp.float32
BF16 = jnp.bfloat16

ROWS = 128
DS = 3584
PR = 112
PC = 512
DT = 4096
FX = 1024
WZ = 512
WX = FX - WZ
HALF = DS // 2
YR = DS // 4
N_MSG = 96


def kernel(
    hid, gain, proj, teach,
    loss_out, hid_out, proj_out, gain_out,
    norm_all, norm_t, proj_full,
    t_ma, t_mb, t_own, t_z,
    z_in, x_fl, x_fr, x_gl, x_gr, x_sum, z_in2, s_fl, s_fr, s_gl, s_gr,
    pred, pgrad,
    pg, c_in, y_fl, y_fr, y_gl, y_gr, y_sum, zp_in, zm_in,
    ng, n_fl, n_fr, n_gl, n_gr,
    acc, red_c, red_x, red_y, red_z,
    send_sem, recv_sem, local_sem,
):
    dp = lax.axis_index("dp")
    tp = lax.axis_index("tensor")
    y, zh, c = dp // 8, (dp // 2) % 4, dp % 2
    x, zl = tp // 2, tp % 2
    z = zh * 2 + zl

    def device(y=y, z=z, c=c, x=x):
        return ((y * 4 + z // 2) * 2 + c, x * 2 + z % 2)

    def xp(d):
        return (x + d) % 4

    def yp(d):
        return (y + d) % 4

    def zp(d):
        return (z + d) % 8

    right, left = device(x=xp(1)), device(x=xp(3))
    up, down = device(y=yp(1)), device(y=yp(3))
    above, below = device(z=zp(1)), device(z=zp(7))
    mate = device(c=1 - c)
    pair = device(z=z + 1 - 2 * zl)

    opened = []

    def send(src, dst, dev):
        i = len(opened)
        copy = pltpu.make_async_remote_copy(
            src_ref=src, dst_ref=dst, send_sem=send_sem.at[i], recv_sem=recv_sem.at[i],
            device_id=dev, device_id_type=MESH,
        )
        copy.start()
        opened.append(copy)
        return copy

    def fetch(src, dst, i):
        copy = pltpu.make_async_copy(src, dst, local_sem.at[i])
        copy.start()
        return copy

    def merge(out, parts, n):
        def step(i, _):
            total = parts[0][i].astype(F32)
            for part in parts[1:]:
                total = total + part[i].astype(F32)
            out[i] = total.astype(out.dtype)
            return 0
        lax.fori_loop(0, n, step, 0)

    def merge_rows(out, parts, n):
        def step(i, _):
            rows = pl.ds(pl.multiple_of(i * 16, 16), 16)
            total = parts[0][rows, :].astype(F32)
            for part in parts[1:]:
                total = total + part[rows, :].astype(F32)
            out[rows, :] = total.astype(out.dtype)
            return 0
        lax.fori_loop(0, n // 16, step, 0)

    partners = [mate]
    partners += [device(x=xp(d)) for d in (1, 2, 3)]
    partners += [device(y=yp(d)) for d in (1, 2, 3)]
    partners += [device(z=zp(d)) for d in range(1, 8)]
    barrier = pltpu.get_barrier_semaphore()
    for dev in partners:
        pl.semaphore_signal(barrier, inc=1, device_id=dev, device_id_type=MESH)
    pl.semaphore_wait(barrier, len(partners))

    def cols_x(d):
        return pl.ds(pl.multiple_of(xp(d) * FX + WZ, 128), WX)

    def cols_z(d):
        return pl.ds(pl.multiple_of(xp(d) * FX, 128), WZ)

    x_fwd_r = send(teach.at[:, 0, :, cols_x(2)], x_fl, right)
    x_fwd_l = send(teach.at[:, 1, :, cols_x(2)], x_fr, left)
    def pblock(zz):
        return proj_full.at[y, zz // 2, c, :, pl.ds(pl.multiple_of((zz % 2) * PC, PC), PC)]

    z_up = send(proj, pblock(z), above)
    z_dn = send(proj, pblock(z), below)
    own = pltpu.make_async_copy(proj, pblock(z), local_sem.at[0])
    own.start()
    order = (2, 1, 3, 0)
    z_msgs = [
        send(teach.at[:, 1 - zl, :, cols_z(d)], z_in.at[k], pair) for k, d in enumerate(order)
    ]
    loads = [
        fetch(teach.at[:, 0, :, cols_x(1)], t_ma, 1),
        fetch(teach.at[:, 1, :, cols_x(3)], t_mb, 2),
        fetch(teach.at[:, :, :, cols_x(0)], t_own, 3),
    ]
    loads_z = [
        fetch(teach.at[:, zl, :, cols_z(d)], t_z.at[k], 4 + k) for k, d in enumerate(order)
    ]

    def norm_step(i, _):
        rows = pl.ds(pl.multiple_of(i * 16, 16), 16)
        h = hid[rows, :].astype(F32)
        inv = lax.rsqrt(jnp.mean(h * h, axis=1, keepdims=True) + epsilon)
        norm_all[x, rows, :] = (h * inv * gain[...]).astype(BF16)
        return 0

    lax.fori_loop(0, ROWS // 16, norm_step, 0)
    n_r = send(norm_all.at[x], norm_all.at[x], right)
    n_l = send(norm_all.at[x], norm_all.at[x], left)
    x_dir_r = send(teach.at[:, 1, :, cols_x(1)], x_gl.at[1], right)
    x_dir_l = send(teach.at[:, 0, :, cols_x(3)], x_gr.at[0], left)

    ups, dns = [z_up], [z_dn]
    for s in range(1, 4):
        ups[-1].wait_recv()
        ups.append(send(pblock(zp(8 - s)), pblock(zp(8 - s)), above))
        dns[-1].wait_recv()
        if s < 3:
            dns.append(send(pblock(zp(s)), pblock(zp(s)), below))
    ups[-1].wait_recv()
    own.wait()
    y_up = send(proj_full.at[y, :, c], proj_full.at[y, :, c], up)
    y_dn = send(proj_full.at[y, :, c], proj_full.at[y, :, c], down)
    core = [send(proj_full.at[y, :, c], proj_full.at[y, :, c], mate)]

    x_fwd_r.wait_recv()
    loads[0].wait()
    merge(t_ma, (t_ma, x_fl), 4)
    x_mrg_r = send(t_ma, x_gl.at[0], right)
    x_fwd_l.wait_recv()
    loads[1].wait()
    merge(t_mb, (t_mb, x_fr), 4)
    x_mrg_l = send(t_mb, x_gr.at[1], left)

    lo, hi = pl.ds(0, ROWS // 2), pl.ds(ROWS // 2, ROWS // 2)
    n_r.wait_recv()
    n_r2 = send(norm_all.at[xp(3), lo], norm_all.at[xp(3), lo], right)
    n_l.wait_recv()
    n_l2 = send(norm_all.at[xp(1), hi], norm_all.at[xp(1), hi], left)

    z_msgs[0].wait_recv()
    loads_z[0].wait()
    merge(t_z.at[0], (t_z.at[0], z_in.at[0]), 4)
    a, b = pl.ds(0, 2), pl.ds(2, 2)
    s_fwd_r = send(t_z.at[0, a], s_fl, right)
    s_fwd_l = send(t_z.at[0, b], s_fr, left)

    y_up.wait_recv()
    y_up2 = send(proj_full.at[yp(3), a, c], proj_full.at[yp(3), a, c], up)
    core.append(send(proj_full.at[yp(3), :, c], proj_full.at[yp(3), :, c], mate))
    y_dn.wait_recv()
    y_dn2 = send(proj_full.at[yp(1), b, c], proj_full.at[yp(1), b, c], down)
    core.append(send(proj_full.at[yp(1), :, c], proj_full.at[yp(1), :, c], mate))

    z_msgs[1].wait_recv()
    loads_z[1].wait()
    merge(t_z.at[1], (t_z.at[1], z_in.at[1]), 4)
    s_dir_r = send(t_z.at[1, b], s_gl.at[b], right)
    z_msgs[2].wait_recv()
    loads_z[2].wait()
    merge(t_z.at[2], (t_z.at[2], z_in.at[2]), 4)
    s_dir_l = send(t_z.at[2, a], s_gr.at[a], left)
    s_fwd_r.wait_recv()
    merge(t_z.at[1, a], (t_z.at[1, a], s_fl), 2)
    s_mrg_r = send(t_z.at[1, a], s_gl.at[a], right)
    s_fwd_l.wait_recv()
    merge(t_z.at[2, b], (t_z.at[2, b], s_fr), 2)
    s_mrg_l = send(t_z.at[2, b], s_gr.at[b], left)

    for copy in (x_dir_r, x_dir_l, x_mrg_r, x_mrg_l):
        copy.wait_recv()
    loads[2].wait()

    def x_step(i, _):
        for t in range(2):
            total = t_own[i, t].astype(F32) + x_gl[t, i].astype(F32) + x_gr[t, i].astype(F32)
            x_sum[t, i] = total.astype(BF16)
        return 0

    lax.fori_loop(0, 4, x_step, 0)
    z_msg2 = send(x_sum.at[1 - zl], z_in2, pair)

    y_up2.wait_recv()
    y_dn2.wait_recv()
    core.append(send(proj_full.at[yp(2), :, c], proj_full.at[yp(2), :, c], mate))
    n_r2.wait_recv()
    n_l2.wait_recv()

    def transpose_step(i, _):
        cols = pl.ds(pl.multiple_of(i * 512, 512), 512)
        for t in range(4):
            norm_t[cols, t * ROWS:(t + 1) * ROWS] = norm_all[t, :, cols].T
        return 0

    lax.fori_loop(0, DS // 512, transpose_step, 0)
    for copy in core:
        copy.wait_recv()

    def pred_step(i, _):
        cols = pl.ds(pl.multiple_of(i * 256, 256), 256)
        left_part = norm_all[...].reshape(4 * ROWS, DS)
        right_part = proj_full[:, :, :, :, cols].reshape(DS, 256)
        pred[:, cols] = jnp.dot(left_part, right_part, preferred_element_type=F32).astype(BF16)
        return 0

    lax.fori_loop(0, FX // 256, pred_step, 0)

    z_msgs[3].wait_recv()
    loads_z[3].wait()
    for copy in (s_dir_r, s_dir_l, s_mrg_r, s_mrg_l):
        copy.wait_recv()
    z_msg2.wait_recv()

    def miss_step(i, loss):
        t, r = i // 8, i % 8
        rows = pl.ds(pl.multiple_of(r * 16, 16), 16)
        out_rows = pl.ds(pl.multiple_of(i * 16, 16), 16)
        target = (t_z[3, t, rows, :].astype(F32) + z_in[3, t, rows, :].astype(F32)
                  + s_gl[t, rows, :].astype(F32) + s_gr[t, rows, :].astype(F32))
        miss = pred[out_rows, :WZ].astype(F32) - target
        pgrad[out_rows, :WZ] = miss.astype(BF16)
        loss = loss + jnp.sum(miss * miss, axis=0, keepdims=True)[:, :512]
        target = x_sum[zl, t, rows, :].astype(F32) + z_in2[t, rows, :].astype(F32)
        miss = pred[out_rows, WZ:].astype(F32) - target
        pgrad[out_rows, WZ:] = miss.astype(BF16)
        return loss + jnp.sum(miss * miss, axis=0, keepdims=True)

    loss = lax.fori_loop(0, 32, miss_step, jnp.zeros((1, 512), F32))
    loss = jnp.sum(loss, axis=1, keepdims=True)

    def pgrad_block(yy):
        rows = pl.ds(pl.multiple_of(yy * YR, 128), YR)

        def step(i, _):
            cols = pl.ds(pl.multiple_of(i * 256, 256), 256)
            part = jnp.dot(norm_t[rows, :], pgrad[:, cols], preferred_element_type=F32)
            pg[yy, :, :, :, cols] = part.astype(BF16).reshape(4, 2, PR, 256)
            return 0

        lax.fori_loop(0, FX // 256, step, 0)
        return send(pg.at[yy, :, 1 - c], c_in.at[yy], mate)

    def core_merge(copy, yy):
        copy.wait_recv()
        merge(c_in.at[yy], (c_in.at[yy], pg.at[yy, :, c]), 4)

    y2, y1, y3 = yp(2), yp(1), yp(3)
    c_2 = pgrad_block(y2)
    c_1 = pgrad_block(y1)
    core_merge(c_2, y2)
    y_fwd_u = send(c_in.at[y2, a], y_fl, up)
    y_fwd_d = send(c_in.at[y2, b], y_fr, down)
    c_3 = pgrad_block(y3)
    core_merge(c_1, y1)
    y_dir_u = send(c_in.at[y1, b], y_gl.at[b], up)
    c_0 = pgrad_block(y)
    core_merge(c_3, y3)
    y_dir_d = send(c_in.at[y3, a], y_gr.at[a], down)

    def ngrad_half(k):
        def step(i, _):
            weights = proj_full[2 * k:2 * k + 2].reshape(HALF, FX)
            rows = pl.ds(pl.multiple_of(i * 256, 256), 256)
            part = lax.dot_general(pgrad[rows, :], weights, (((1,), (1,)), ((), ())),
                                   preferred_element_type=F32)
            ng[pl.ds(i * 2, 2), :, k * HALF:(k + 1) * HALF] = (
                part.astype(BF16).reshape(2, ROWS, HALF))
            return 0

        lax.fori_loop(0, 2, step, 0)

    ca, cb = pl.ds(0, HALF), pl.ds(HALF, HALF)
    ngrad_half(0)
    n_fwd_r = send(ng.at[xp(2), :, ca], n_fl, right)
    n_dir_l = send(ng.at[xp(3), :, ca], n_gr.at[:, ca], left)
    y_fwd_u.wait_recv()
    merge(c_in.at[y1, a], (c_in.at[y1, a], y_fl), 2)
    y_mrg_u = send(c_in.at[y1, a], y_gl.at[a], up)
    y_fwd_d.wait_recv()
    merge(c_in.at[y3, b], (c_in.at[y3, b], y_fr), 2)
    y_mrg_d = send(c_in.at[y3, b], y_gr.at[b], down)
    ngrad_half(1)
    n_fwd_l = send(ng.at[xp(2), :, cb], n_fr, left)
    n_dir_r = send(ng.at[xp(1), :, cb], n_gl.at[:, cb], right)
    core_merge(c_0, y)
    n_fwd_r.wait_recv()
    merge_rows(ng.at[xp(1), :, ca], (ng.at[xp(1), :, ca], n_fl), ROWS)
    n_mrg_r = send(ng.at[xp(1), :, ca], n_gl.at[:, ca], right)
    n_fwd_l.wait_recv()
    merge_rows(ng.at[xp(3), :, cb], (ng.at[xp(3), :, cb], n_fr), ROWS)
    n_mrg_l = send(ng.at[xp(3), :, cb], n_gr.at[:, cb], left)

    for copy in (y_dir_u, y_dir_d, y_mrg_u, y_mrg_d):
        copy.wait_recv()
    merge(y_sum, (c_in.at[y], y_gl, y_gr), 4)

    def sblock(d):
        zz = zp(d)
        return y_sum.at[zz // 2, :, pl.ds(pl.multiple_of((zz % 2) * PC, PC), PC)]

    def add_block(out, block):
        out[...] = (out[...].astype(F32) + block[...].astype(F32)).astype(BF16)

    u1 = send(sblock(3), zp_in.at[0], above)
    d1 = send(sblock(4), zm_in.at[0], below)
    u1.wait_recv()
    add_block(zp_in.at[0], sblock(2))
    u2 = send(zp_in.at[0], zp_in.at[1], above)
    d1.wait_recv()
    add_block(zm_in.at[0], sblock(5))
    d2 = send(zm_in.at[0], zm_in.at[1], below)
    u2.wait_recv()
    add_block(zp_in.at[1], sblock(1))
    u3 = send(zp_in.at[1], zp_in.at[2], above)
    d2.wait_recv()
    add_block(zm_in.at[1], sblock(6))
    d3 = send(zm_in.at[1], zm_in.at[2], below)
    d3.wait_recv()
    add_block(zm_in.at[2], sblock(7))
    d4 = send(zm_in.at[2], zm_in.at[3], below)

    for copy in (n_dir_r, n_dir_l, n_mrg_r, n_mrg_l):
        copy.wait_recv()

    def hid_step(i, gain_sum):
        rows = pl.ds(pl.multiple_of(i * 16, 16), 16)
        g = ng[x, rows, :].astype(F32) + n_gl[rows, :].astype(F32) + n_gr[rows, :].astype(F32)
        h = hid[rows, :].astype(F32)
        inv = lax.rsqrt(jnp.mean(h * h, axis=1, keepdims=True) + epsilon)
        scaled = h * inv
        gain_sum = gain_sum + jnp.sum(g * scaled, axis=0, keepdims=True)
        g = g * gain[...]
        mean = jnp.mean(g * scaled, axis=1, keepdims=True)
        hid_out[rows, :] = (inv * (g - scaled * mean)).astype(BF16)
        return gain_sum

    gain_sum = lax.fori_loop(0, ROWS // 16, hid_step, jnp.zeros((1, DS), F32))

    u3.wait_recv()
    d4.wait_recv()
    total = (sblock(0)[...].astype(F32) + zp_in[2].astype(F32) + zm_in[3].astype(F32))
    proj_out[...] = total
    squares = jnp.sum(jnp.sum(total * total, axis=0, keepdims=True), axis=1, keepdims=True)

    for i in range(28):
        acc[i:i + 1, :] = gain_sum[:, i * 128:(i + 1) * 128]
    acc[28:29, :] = jnp.broadcast_to(loss, (1, 128))
    acc[29:30, :] = jnp.broadcast_to(squares, (1, 128))
    acc[30:32, :] = jnp.zeros((2, 128), F32)

    def reduce_axis(slots, n, index, dev_at):
        slots[index] = acc[...]
        copies = [send(acc, slots.at[index], dev_at(d)) for d in range(1, n)]
        for copy in copies:
            copy.wait_recv()
        total = slots[0]
        for i in range(1, n):
            total = total + slots[i]
        for copy in copies:
            copy.wait_send()
        acc[...] = total

    reduce_axis(red_c, 2, c, lambda d: mate)
    reduce_axis(red_x, 4, x, lambda d: device(x=xp(d)))
    reduce_axis(red_y, 4, y, lambda d: device(y=yp(d)))
    reduce_axis(red_z, 8, z, lambda d: device(z=zp(d)))
    n_small = 1 + 3 + 3 + 7

    gain_grad = acc[0:28, :]
    gain_squares = jnp.sum(jnp.sum(gain_grad * gain_grad, axis=0, keepdims=True), axis=1, keepdims=True)
    all_squares = acc[29:30, 0:1] + gain_squares
    factor = lax.rsqrt(all_squares / (DS * DT + DS) + epsilon)
    proj_out[...] = proj_out[...] * factor
    gain_out[...] = gain_grad * factor
    loss_out[...] = acc[28:29, :] / (32768 * DT)

    for copy in opened[:len(opened) - n_small]:
        copy.wait_send()


def shards(student_hidden, norm_gain, projection, teacher_terms):
    teach = teacher_terms.reshape(4, 2, ROWS, DT)
    vmem = pl.BlockSpec(memory_space=pltpu.VMEM)
    V = pltpu.VMEM
    loss, hidden_grad, projection_update, gain_update = pl.pallas_call(
        kernel,
        out_shape=(
            jax.ShapeDtypeStruct((1, 128), F32),
            jax.ShapeDtypeStruct((ROWS, DS), BF16),
            jax.ShapeDtypeStruct((PR, PC), F32),
            jax.ShapeDtypeStruct((28, 128), F32),
        ),
        in_specs=[vmem, vmem, vmem, pl.BlockSpec(memory_space=pl.ANY)],
        out_specs=(vmem,) * 4,
        scratch_shapes=[
            V((4, ROWS, DS), BF16), V((DS, 4 * ROWS), BF16), V((4, 4, 2, PR, FX), BF16),
            V((4, ROWS, WX), BF16), V((4, ROWS, WX), BF16), V((4, 2, ROWS, WX), BF16),
            V((4, 4, ROWS, WZ), BF16),
            V((4, 4, ROWS, WZ), BF16),
            V((4, ROWS, WX), BF16), V((4, ROWS, WX), BF16),
            V((2, 4, ROWS, WX), BF16), V((2, 4, ROWS, WX), BF16), V((2, 4, ROWS, WX), BF16),
            V((4, ROWS, WX), BF16),
            V((2, ROWS, WZ), BF16), V((2, ROWS, WZ), BF16),
            V((4, ROWS, WZ), BF16), V((4, ROWS, WZ), BF16),
            V((4 * ROWS, FX), BF16), V((4 * ROWS, FX), BF16),
            V((4, 4, 2, PR, FX), BF16), V((4, 4, PR, FX), BF16),
            V((2, PR, FX), BF16), V((2, PR, FX), BF16),
            V((4, PR, FX), BF16), V((4, PR, FX), BF16), V((4, PR, FX), BF16),
            V((3, PR, PC), BF16), V((4, PR, PC), BF16),
            V((4, ROWS, DS), BF16), V((ROWS, HALF), BF16), V((ROWS, HALF), BF16),
            V((ROWS, DS), BF16), V((ROWS, DS), BF16),
            V((32, 128), F32), V((2, 32, 128), F32), V((4, 32, 128), F32),
            V((4, 32, 128), F32), V((8, 32, 128), F32),
            pltpu.SemaphoreType.DMA((N_MSG,)), pltpu.SemaphoreType.DMA((N_MSG,)),
            pltpu.SemaphoreType.DMA((8,)),
        ],
        compiler_params=pltpu.CompilerParams(
            collective_id=0, has_side_effects=True, vmem_limit_bytes=62 * 1024 * 1024
        ),
    )(student_hidden, norm_gain.reshape(1, DS), projection, teach)
    return loss[0, 0], hidden_grad, projection_update, gain_update.reshape(DS)


def solution(mesh):
    in_specs = (P(("dp", "tensor"), None), P(), P("dp", "tensor"), P("tensor", "dp", None))
    out_specs = (P(), P(("dp", "tensor"), None), P("dp", "tensor"), P())
    return jax.shard_map(shards, mesh=mesh, in_specs=in_specs, out_specs=out_specs, check_vma=False)
```

```python
import jax
import jax.numpy as jnp
from jax import lax
from jax.experimental import pallas as pl
from jax.experimental.pallas import tpu as pltpu
from jax.sharding import PartitionSpec as P

epsilon = 1e-06
MESH = pl.DeviceIdType.MESH
F32 = jnp.float32
BF16 = jnp.bfloat16

ROWS = 128
DS = 3584
PR = 112
PC = 512
DT = 4096
FX = 1024
HP = 256
HALF = DS // 2
YR = DS // 4
N_MSG = 160


def kernel(
    hid, gain, proj, teach,
    loss_out, hid_out, proj_out, gain_out,
    norm_all, norm_t, proj_full,
    t_ma, t_mb, t_own, t_z,
    z_in, x_fl, x_fr, x_gl, x_gr, x_sum, z_in2, s_fl, s_fr, s_gl, s_gr,
    pred, pgrad,
    pg, c_in, y_fl, y_fr, y_gl, y_gr, y_sum, zd_in,
    ng, n_fl, n_fr, n_gl, n_gr,
    acc, red_1, red_2,
    send_sem, recv_sem, local_sem,
):
    dp = lax.axis_index("dp")
    tp = lax.axis_index("tensor")
    y, zh, c = dp // 8, (dp // 2) % 4, dp % 2
    x, zl = tp // 2, tp % 2
    z = zh * 2 + zl

    def device(y=y, z=z, c=c, x=x):
        return ((y * 4 + z // 2) * 2 + c, x * 2 + z % 2)

    def xp(d):
        return (x + d) % 4

    def yp(d):
        return (y + d) % 4

    def zp(d):
        return (z + d) % 8

    right, left = device(x=xp(1)), device(x=xp(3))
    up, down = device(y=yp(1)), device(y=yp(3))
    above, below = device(z=zp(1)), device(z=zp(7))
    mate = device(c=1 - c)
    pair = device(z=z + 1 - 2 * zl)

    opened = []

    def send(src, dst, dev):
        i = len(opened)
        copy = pltpu.make_async_remote_copy(
            src_ref=src, dst_ref=dst, send_sem=send_sem.at[i], recv_sem=recv_sem.at[i],
            device_id=dev, device_id_type=MESH,
        )
        copy.start()
        opened.append(copy)
        return copy

    n_local = [0]

    def fetch(src, dst):
        copy = pltpu.make_async_copy(src, dst, local_sem.at[n_local[0]])
        n_local[0] += 1
        copy.start()
        return copy

    def arrived(*copies):
        for copy in copies:
            copy.wait_recv()

    def merge(out, parts, n):
        def step(i, _):
            total = parts[0][i].astype(F32)
            for part in parts[1:]:
                total = total + part[i].astype(F32)
            out[i] = total.astype(out.dtype)
            return 0
        lax.fori_loop(0, n, step, 0)

    def merge_rows(out, parts, n):
        def step(i, _):
            rows = pl.ds(pl.multiple_of(i * 16, 16), 16)
            total = parts[0][rows, :].astype(F32)
            for part in parts[1:]:
                total = total + part[rows, :].astype(F32)
            out[rows, :] = total.astype(out.dtype)
            return 0
        lax.fori_loop(0, n // 16, step, 0)

    group_1 = [(dc, dz) for dc in range(2) for dz in range(8) if dc or dz]
    group_2 = [(dx, dy) for dx in range(4) for dy in range(4) if dx or dy]
    peers_1 = [device(c=(c + dc) % 2, z=zp(dz)) for dc, dz in group_1]
    peers_2 = [device(x=xp(dx), y=yp(dy)) for dx, dy in group_2]
    barrier = pltpu.get_barrier_semaphore()
    for dev in peers_1 + peers_2:
        pl.semaphore_signal(barrier, inc=1, device_id=dev, device_id_type=MESH)
    pl.semaphore_wait(barrier, len(peers_1) + len(peers_2))

    def tcols(d, part, k):
        return pl.ds(pl.multiple_of(xp(d) * FX + k * PC + part * HP, HP), HP)

    def raw(t, d, part, dst, dev):
        return [send(teach.at[:, t, :, tcols(d, part, k)], dst.at[:, :, pl.ds(k * HP, HP)], dev)
                for k in range(2)]

    def load(t, d, part, dst):
        return [fetch(teach.at[:, t, :, tcols(d, part, k)], dst.at[:, :, pl.ds(k * HP, HP)])
                for k in range(2)]

    def pblock(zz):
        return proj_full.at[y, zz // 2, c, :, pl.ds(pl.multiple_of((zz % 2) * PC, PC), PC)]

    ups = [send(proj, pblock(z), above)]
    dns = [send(proj, pblock(z), below)]
    x_fwd_r = raw(0, 2, 1, x_fl, right)
    x_fwd_l = raw(1, 2, 1, x_fr, left)
    order = (2, 1, 3, 0)
    z_msgs = [raw(1 - zl, 2, 0, z_in.at[0], pair)]
    own = fetch(proj, pblock(z))
    load_ma = load(0, 1, 1, t_ma)
    load_mb = load(1, 3, 1, t_mb)
    load_z = [load(zl, d, 0, t_z.at[k]) for k, d in enumerate(order)]
    load_own = load(0, 0, 1, t_own.at[0]) + load(1, 0, 1, t_own.at[1])

    def norm_step(i, _):
        rows = pl.ds(pl.multiple_of(i * 16, 16), 16)
        h = hid[rows, :].astype(F32)
        inv = lax.rsqrt(jnp.mean(h * h, axis=1, keepdims=True) + epsilon)
        norm_all[x, rows, :] = (h * inv * gain[...]).astype(BF16)
        return 0

    lax.fori_loop(0, ROWS // 16, norm_step, 0)
    n_r = send(norm_all.at[x], norm_all.at[x], right)
    n_l = send(norm_all.at[x], norm_all.at[x], left)

    for s in range(1, 4):
        ups[-1].wait_recv()
        ups.append(send(pblock(zp(8 - s)), pblock(zp(8 - s)), above))
        dns[-1].wait_recv()
        if s < 3:
            dns.append(send(pblock(zp(s)), pblock(zp(s)), below))
    z_msgs.append(raw(1 - zl, 1, 0, z_in.at[1], pair))
    ups[-1].wait_recv()
    own.wait()
    y_up = send(proj_full.at[y, :, c], proj_full.at[y, :, c], up)
    y_dn = send(proj_full.at[y, :, c], proj_full.at[y, :, c], down)
    core = [send(proj_full.at[y, :, c], proj_full.at[y, :, c], mate)]
    z_msgs.append(raw(1 - zl, 3, 0, z_in.at[2], pair))

    arrived(*x_fwd_r)
    for copy in load_ma:
        copy.wait()
    merge(t_ma, (t_ma, x_fl), 4)
    x_last = [send(t_ma, x_gl.at[0], right)]
    arrived(*x_fwd_l)
    for copy in load_mb:
        copy.wait()
    merge(t_mb, (t_mb, x_fr), 4)
    x_last += [send(t_mb, x_gr.at[1], left)]
    x_last += raw(1, 1, 1, x_gl.at[1], right)
    x_last += raw(0, 3, 1, x_gr.at[0], left)

    a, b = pl.ds(0, 2), pl.ds(2, 2)

    def z_merge(k):
        arrived(*z_msgs[k])
        for copy in load_z[k]:
            copy.wait()
        merge(t_z.at[k], (t_z.at[k], z_in.at[k]), 4)

    z_merge(0)
    s_fwd_r = send(t_z.at[0, a], s_fl, right)
    s_fwd_l = send(t_z.at[0, b], s_fr, left)
    z_msgs.append(raw(1 - zl, 0, 0, z_in.at[3], pair))

    lo, hi = pl.ds(0, ROWS // 2), pl.ds(ROWS // 2, ROWS // 2)
    n_r.wait_recv()
    n_r2 = send(norm_all.at[xp(3), lo], norm_all.at[xp(3), lo], right)
    n_l.wait_recv()
    n_l2 = send(norm_all.at[xp(1), hi], norm_all.at[xp(1), hi], left)

    z_merge(1)
    s_last = [send(t_z.at[1, b], s_gl.at[b], right)]
    z_merge(2)
    s_last += [send(t_z.at[2, a], s_gr.at[a], left)]

    y_up.wait_recv()
    y_up2 = send(proj_full.at[yp(3), a, c], proj_full.at[yp(3), a, c], up)
    core.append(send(proj_full.at[yp(3), :, c], proj_full.at[yp(3), :, c], mate))
    y_dn.wait_recv()
    y_dn2 = send(proj_full.at[yp(1), b, c], proj_full.at[yp(1), b, c], down)
    core.append(send(proj_full.at[yp(1), :, c], proj_full.at[yp(1), :, c], mate))

    s_fwd_r.wait_recv()
    merge(t_z.at[1, a], (t_z.at[1, a], s_fl), 2)
    s_last += [send(t_z.at[1, a], s_gl.at[a], right)]
    s_fwd_l.wait_recv()
    merge(t_z.at[2, b], (t_z.at[2, b], s_fr), 2)
    s_last += [send(t_z.at[2, b], s_gr.at[b], left)]

    arrived(*x_last)
    for copy in load_own:
        copy.wait()
    for t in range(2):
        merge(x_sum.at[t], (t_own.at[t], x_gl.at[t], x_gr.at[t]), 4)
    z_msg2 = send(x_sum.at[1 - zl], z_in2, pair)

    y_up2.wait_recv()
    y_dn2.wait_recv()
    core.append(send(proj_full.at[yp(2), :, c], proj_full.at[yp(2), :, c], mate))
    arrived(n_r2, n_l2)

    def transpose_step(i, _):
        cols = pl.ds(pl.multiple_of(i * 512, 512), 512)
        for t in range(4):
            norm_t[cols, t * ROWS:(t + 1) * ROWS] = norm_all[t, :, cols].T
        return 0

    lax.fori_loop(0, DS // 512, transpose_step, 0)
    arrived(*core)

    def pred_part(part):
        def step(k, _):
            cols = pl.ds(pl.multiple_of(k * PC + part * HP, HP), HP)
            out_cols = pl.ds(pl.multiple_of(part * PC + k * HP, HP), HP)
            rows_part = norm_all[...].reshape(4 * ROWS, DS)
            cols_part = proj_full[:, :, :, :, cols].reshape(DS, HP)
            product = jnp.dot(rows_part, cols_part, preferred_element_type=F32)
            pred[:, out_cols] = product.astype(BF16)
            return 0

        lax.fori_loop(0, 2, step, 0)

    def mismatch_part(part, terms):
        cols = slice(part * PC, part * PC + PC)

        def step(i, loss):
            t = i // 8
            rows = pl.ds(pl.multiple_of((i % 8) * 16, 16), 16)
            out_rows = pl.ds(pl.multiple_of(i * 16, 16), 16)
            target = terms[0][t, rows, :].astype(F32)
            for term in terms[1:]:
                target = target + term[t, rows, :].astype(F32)
            miss = pred[out_rows, cols].astype(F32) - target
            pgrad[out_rows, cols] = miss.astype(BF16)
            return loss + jnp.sum(miss * miss, axis=0, keepdims=True)

        return lax.fori_loop(0, 32, step, jnp.zeros((1, PC), F32))

    def ngrad_half(part, k):
        def step(i, _):
            yy = 2 * k + i
            cols = pl.ds(pl.multiple_of(yy * YR, 128), YR)
            total = jnp.zeros((4 * ROWS, YR), F32)
            for m in range(2):
                weights = proj_full[yy, :, :, :, m * PC + part * HP:m * PC + part * HP + HP]
                total = total + lax.dot_general(
                    pgrad[:, part * PC + m * HP:part * PC + m * HP + HP],
                    weights.reshape(YR, HP), (((1,), (1,)), ((), ())),
                    preferred_element_type=F32)
            total = total.reshape(4, ROWS, YR)
            if part == 0:
                total = total + ng[:, :, cols].astype(F32)
            ng[:, :, cols] = total.astype(BF16)
            return 0

        lax.fori_loop(0, 2, step, 0)

    y2, y1, y3 = yp(2), yp(1), yp(3)

    def pgrad_sends(part):
        def block(yy):
            rows = pl.ds(pl.multiple_of(yy * YR, 128), YR)

            def step(k, _):
                cols = pl.ds(pl.multiple_of(part * PC + k * HP, HP), HP)
                product = jnp.dot(norm_t[rows, :], pgrad[:, cols], preferred_element_type=F32)
                pg[part, yy, :, :, :, pl.ds(pl.multiple_of(k * HP, HP), HP)] = (
                    product.astype(BF16).reshape(4, 2, PR, HP))
                return 0

            lax.fori_loop(0, 2, step, 0)
            return send(pg.at[part, yy, :, 1 - c], c_in.at[part, yy], mate)

        def core_merge(copy, yy):
            copy.wait_recv()
            merge(c_in.at[part, yy], (c_in.at[part, yy], pg.at[part, yy, :, c]), 4)

        c_2 = block(y2)
        c_1 = block(y1)
        core_merge(c_2, y2)
        fwd_u = send(c_in.at[part, y2, a], y_fl.at[part], up)
        fwd_d = send(c_in.at[part, y2, b], y_fr.at[part], down)
        c_3 = block(y3)
        core_merge(c_1, y1)
        dir_u = send(c_in.at[part, y1, b], y_gl.at[part, b], up)
        c_0 = block(y)
        core_merge(c_3, y3)
        dir_d = send(c_in.at[part, y3, a], y_gr.at[part, a], down)
        core_merge(c_0, y)
        return fwd_u, fwd_d, dir_u, dir_d

    def y_merge(part, fwd_u, fwd_d, dir_u, dir_d):
        fwd_u.wait_recv()
        merge(c_in.at[part, y1, a], (c_in.at[part, y1, a], y_fl.at[part]), 2)
        mrg_u = send(c_in.at[part, y1, a], y_gl.at[part, a], up)
        fwd_d.wait_recv()
        merge(c_in.at[part, y3, b], (c_in.at[part, y3, b], y_fr.at[part]), 2)
        mrg_d = send(c_in.at[part, y3, b], y_gr.at[part, b], down)
        return dir_u, dir_d, mrg_u, mrg_d

    def sblock(part, d):
        zz = zp(d)
        return y_sum.at[part, zz // 2, :, pl.ds(pl.multiple_of((zz % 2) * HP, HP), HP)]

    def z_sends(part, copies):
        arrived(*copies)
        merge(y_sum.at[part], (c_in.at[part, y], y_gl.at[part], y_gr.at[part]), 4)
        return [send(sblock(part, d), zd_in.at[part, d - 1], device(z=zp(d)))
                for d in (4, 3, 5, 2, 6, 1, 7)]

    pred_part(1)
    z_msg2.wait_recv()
    loss = mismatch_part(1, (x_sum.at[zl], z_in2))
    y_part1 = pgrad_sends(1)
    pred_part(0)
    ngrad_half(1, 0)
    ngrad_half(1, 1)
    y_part1 = y_merge(1, *y_part1)

    arrived(*z_msgs[3])
    for copy in load_z[3]:
        copy.wait()
    arrived(*s_last)
    loss = loss + mismatch_part(0, (t_z.at[3], z_in.at[3], s_gl, s_gr))
    loss = jnp.sum(loss, axis=1, keepdims=True)
    ca, cb = pl.ds(0, HALF), pl.ds(HALF, HALF)
    ngrad_half(0, 0)
    n_fwd_r = send(ng.at[xp(2), :, ca], n_fl, right)
    n_last = [send(ng.at[xp(3), :, ca], n_gr.at[:, ca], left)]
    ngrad_half(0, 1)
    n_fwd_l = send(ng.at[xp(2), :, cb], n_fr, left)
    n_last += [send(ng.at[xp(1), :, cb], n_gl.at[:, cb], right)]
    y_part0 = pgrad_sends(0)
    z_part1 = z_sends(1, y_part1)
    y_part0 = y_merge(0, *y_part0)
    n_fwd_r.wait_recv()
    merge_rows(ng.at[xp(1), :, ca], (ng.at[xp(1), :, ca], n_fl), ROWS)
    n_last += [send(ng.at[xp(1), :, ca], n_gl.at[:, ca], right)]
    n_fwd_l.wait_recv()
    merge_rows(ng.at[xp(3), :, cb], (ng.at[xp(3), :, cb], n_fr), ROWS)
    n_last += [send(ng.at[xp(3), :, cb], n_gr.at[:, cb], left)]
    z_part0 = z_sends(0, y_part0)

    arrived(*n_last)

    def hid_step(i, gain_sum):
        rows = pl.ds(pl.multiple_of(i * 16, 16), 16)
        g = ng[x, rows, :].astype(F32) + n_gl[rows, :].astype(F32) + n_gr[rows, :].astype(F32)
        h = hid[rows, :].astype(F32)
        inv = lax.rsqrt(jnp.mean(h * h, axis=1, keepdims=True) + epsilon)
        scaled = h * inv
        gain_sum = gain_sum + jnp.sum(g * scaled, axis=0, keepdims=True)
        g = g * gain[...]
        mean = jnp.mean(g * scaled, axis=1, keepdims=True)
        hid_out[rows, :] = (inv * (g - scaled * mean)).astype(BF16)
        return gain_sum

    gain_sum = lax.fori_loop(0, ROWS // 16, hid_step, jnp.zeros((1, DS), F32))

    squares = jnp.zeros((1, 1), F32)
    for part, copies in ((1, z_part1), (0, z_part0)):
        arrived(*copies)
        total = sblock(part, 0)[...].astype(F32)
        for d in range(7):
            total = total + zd_in[part, d].astype(F32)
        proj_out[:, part * HP:part * HP + HP] = total
        squares = squares + jnp.sum(
            jnp.sum(total * total, axis=0, keepdims=True), axis=1, keepdims=True)

    for i in range(28):
        acc[i:i + 1, :] = gain_sum[:, i * 128:(i + 1) * 128]
    acc[28:29, :] = jnp.broadcast_to(loss, (1, 128))
    acc[29:30, :] = jnp.broadcast_to(squares, (1, 128))
    acc[30:32, :] = jnp.zeros((2, 128), F32)
    drained = len(opened)

    def reduce_group(slots, index, peers):
        slots[index] = acc[...]
        copies = [send(acc, slots.at[index], dev) for dev in peers]
        arrived(*copies)
        total = slots[0]
        for i in range(1, 16):
            total = total + slots[i]
        for copy in copies:
            copy.wait_send()
        acc[...] = total

    reduce_group(red_1, c * 8 + z, peers_1)
    reduce_group(red_2, x * 4 + y, peers_2)

    gain_grad = acc[0:28, :]
    gain_squares = jnp.sum(jnp.sum(gain_grad * gain_grad, axis=0, keepdims=True), axis=1, keepdims=True)
    all_squares = acc[29:30, 0:1] + gain_squares
    factor = lax.rsqrt(all_squares / (DS * DT + DS) + epsilon)
    proj_out[...] = proj_out[...] * factor
    gain_out[...] = gain_grad * factor
    loss_out[...] = acc[28:29, :] / (32768 * DT)

    for copy in opened[:drained]:
        copy.wait_send()


def shards(student_hidden, norm_gain, projection, teacher_terms):
    teach = teacher_terms.reshape(4, 2, ROWS, DT)
    vmem = pl.BlockSpec(memory_space=pltpu.VMEM)
    V = pltpu.VMEM
    loss, hidden_grad, projection_update, gain_update = pl.pallas_call(
        kernel,
        out_shape=(
            jax.ShapeDtypeStruct((1, 128), F32),
            jax.ShapeDtypeStruct((ROWS, DS), BF16),
            jax.ShapeDtypeStruct((PR, PC), F32),
            jax.ShapeDtypeStruct((28, 128), F32),
        ),
        in_specs=[vmem, vmem, vmem, pl.BlockSpec(memory_space=pl.ANY)],
        out_specs=(vmem,) * 4,
        scratch_shapes=[
            V((4, ROWS, DS), BF16), V((DS, 4 * ROWS), BF16), V((4, 4, 2, PR, FX), BF16),
            V((4, ROWS, PC), BF16), V((4, ROWS, PC), BF16), V((2, 4, ROWS, PC), BF16),
            V((4, 4, ROWS, PC), BF16),
            V((4, 4, ROWS, PC), BF16),
            V((4, ROWS, PC), BF16), V((4, ROWS, PC), BF16),
            V((2, 4, ROWS, PC), BF16), V((2, 4, ROWS, PC), BF16), V((2, 4, ROWS, PC), BF16),
            V((4, ROWS, PC), BF16),
            V((2, ROWS, PC), BF16), V((2, ROWS, PC), BF16),
            V((4, ROWS, PC), BF16), V((4, ROWS, PC), BF16),
            V((4 * ROWS, FX), BF16), V((4 * ROWS, FX), BF16),
            V((2, 4, 4, 2, PR, PC), BF16), V((2, 4, 4, PR, PC), BF16),
            V((2, 2, PR, PC), BF16), V((2, 2, PR, PC), BF16),
            V((2, 4, PR, PC), BF16), V((2, 4, PR, PC), BF16), V((2, 4, PR, PC), BF16),
            V((2, 7, PR, HP), BF16),
            V((4, ROWS, DS), BF16), V((ROWS, HALF), BF16), V((ROWS, HALF), BF16),
            V((ROWS, DS), BF16), V((ROWS, DS), BF16),
            V((32, 128), F32), V((16, 32, 128), F32), V((16, 32, 128), F32),
            pltpu.SemaphoreType.DMA((N_MSG,)), pltpu.SemaphoreType.DMA((N_MSG,)),
            pltpu.SemaphoreType.DMA((24,)),
        ],
        compiler_params=pltpu.CompilerParams(
            collective_id=0, has_side_effects=True, vmem_limit_bytes=62 * 1024 * 1024
        ),
    )(student_hidden, norm_gain.reshape(1, DS), projection, teach)
    return loss[0, 0], hidden_grad, projection_update, gain_update.reshape(DS)


def solution(mesh):
    in_specs = (P(("dp", "tensor"), None), P(), P("dp", "tensor"), P("tensor", "dp", None))
    out_specs = (P(), P(("dp", "tensor"), None), P("dp", "tensor"), P())
    return jax.shard_map(shards, mesh=mesh, in_specs=in_specs, out_specs=out_specs, check_vma=False)
```

```python
import jax
import jax.numpy as jnp
from jax import lax
from jax.experimental import pallas as pl
from jax.experimental.pallas import tpu as pltpu
from jax.sharding import PartitionSpec as P

epsilon = 1e-06
MESH = pl.DeviceIdType.MESH
F32 = jnp.float32
BF16 = jnp.bfloat16

ROWS = 128
DS = 3584
PR = 112
PC = 512
DT = 4096
FX = 1024
HP = 256
HALF = DS // 2
YR = DS // 4
N_MSG = 160


def kernel(
    hid, gain_in, proj, teach,
    loss_out, hid_out, proj_out, gain_out,
    norm_all, norm_t, proj_full,
    t_ma, t_mb, t_own, t_z,
    z_in, x_fl, x_fr, x_gl, x_gr, x_sum, z_in2, s_fl, s_fr, s_gl, s_gr,
    pred, pgrad,
    pg, c_in, y_fl, y_fr, y_gl, y_gr, y_sum, zd_in,
    ng, n_fl, n_fr, n_gl, n_gr,
    gain, gain_t, m_1, m_2, s_1, s_2,
    send_sem, recv_sem, local_sem,
):
    dp = lax.axis_index("dp")
    tp = lax.axis_index("tensor")
    y, zh, c = dp // 8, (dp // 2) % 4, dp % 2
    x, zl = tp // 2, tp % 2
    z = zh * 2 + zl

    def device(y=y, z=z, c=c, x=x):
        return ((y * 4 + z // 2) * 2 + c, x * 2 + z % 2)

    def xp(d):
        return (x + d) % 4

    def yp(d):
        return (y + d) % 4

    def zp(d):
        return (z + d) % 8

    right, left = device(x=xp(1)), device(x=xp(3))
    up, down = device(y=yp(1)), device(y=yp(3))
    above, below = device(z=zp(1)), device(z=zp(7))
    mate = device(c=1 - c)
    pair = device(z=z + 1 - 2 * zl)

    opened = []

    def send(src, dst, dev):
        i = len(opened)
        copy = pltpu.make_async_remote_copy(
            src_ref=src, dst_ref=dst, send_sem=send_sem.at[i], recv_sem=recv_sem.at[i],
            device_id=dev, device_id_type=MESH,
        )
        copy.start()
        opened.append(copy)
        return copy

    n_local = [0]

    def fetch(src, dst):
        copy = pltpu.make_async_copy(src, dst, local_sem.at[n_local[0]])
        n_local[0] += 1
        copy.start()
        return copy

    def arrived(*copies):
        for copy in copies:
            copy.wait_recv()

    def merge(out, parts, n):
        def step(i, _):
            total = parts[0][i].astype(F32)
            for part in parts[1:]:
                total = total + part[i].astype(F32)
            out[i] = total.astype(out.dtype)
            return 0
        lax.fori_loop(0, n, step, 0)

    def merge_rows(out, parts, n):
        def step(i, _):
            rows = pl.ds(pl.multiple_of(i * 16, 16), 16)
            total = parts[0][rows, :].astype(F32)
            for part in parts[1:]:
                total = total + part[rows, :].astype(F32)
            out[rows, :] = total.astype(out.dtype)
            return 0
        lax.fori_loop(0, n // 16, step, 0)

    def transpose(t):
        out_cols = slice(t * ROWS, t * ROWS + ROWS)

        def step(i, _):
            cols = pl.ds(pl.multiple_of(i * 512, 512), 512)
            norm_t[cols, out_cols] = norm_all[t, :, cols].T
            return 0

        lax.fori_loop(0, DS // 512, step, 0)

    places = (0, 1, 3, 2)

    def pred_part(part, first, end):
        rows = slice(first * ROWS, end * ROWS)

        def step(k, _):
            cols = pl.ds(pl.multiple_of(k * PC + part * HP, HP), HP)
            out_cols = pl.ds(pl.multiple_of(part * PC + k * HP, HP), HP)
            rows_part = norm_all[first:end].reshape((end - first) * ROWS, DS)
            cols_part = proj_full[:, :, :, :, cols].reshape(DS, HP)
            product = jnp.dot(rows_part, cols_part, preferred_element_type=F32)
            pred[rows, out_cols] = product.astype(BF16)
            return 0

        lax.fori_loop(0, 2, step, 0)

    group_1 = [(dc, dz) for dc in range(2) for dz in range(8) if dc or dz]
    group_2 = [(dx, dy) for dx in range(4) for dy in range(4) if dx or dy]
    peers_1 = [device(c=(c + dc) % 2, z=zp(dz)) for dc, dz in group_1]
    peers_2 = [device(x=xp(dx), y=yp(dy)) for dx, dy in group_2]
    barrier = pltpu.get_barrier_semaphore()
    for dev in peers_1 + peers_2:
        pl.semaphore_signal(barrier, inc=1, device_id=dev, device_id_type=MESH)
    pl.semaphore_wait(barrier, len(peers_1) + len(peers_2))

    def tcols(d, part, k):
        return pl.ds(pl.multiple_of(xp(d) * FX + k * PC + part * HP, HP), HP)

    def raw(t, d, part, dst, dev):
        return [send(teach.at[:, t, :, tcols(d, part, k)], dst.at[:, :, pl.ds(k * HP, HP)], dev)
                for k in range(2)]

    def load(t, d, part, dst):
        return [fetch(teach.at[:, t, :, tcols(d, part, k)], dst.at[:, :, pl.ds(k * HP, HP)])
                for k in range(2)]

    def pblock(zz):
        return proj_full.at[y, zz // 2, c, :, pl.ds(pl.multiple_of((zz % 2) * PC, PC), PC)]

    ups = [send(proj, pblock(z), above)]
    dns = [send(proj, pblock(z), below)]
    x_fwd_r = raw(0, 2, 1, x_fl, right)
    x_fwd_l = raw(1, 2, 1, x_fr, left)
    order = (2, 1, 3, 0)
    z_msgs = []
    own = fetch(proj, pblock(z))
    load_ma = load(0, 1, 1, t_ma)
    load_mb = load(1, 3, 1, t_mb)
    load_z = [load(zl, d, 0, t_z.at[k]) for k, d in enumerate(order)]
    load_own = load(0, 0, 1, t_own.at[0]) + load(1, 0, 1, t_own.at[1])

    for i in range(DS // 128):
        gain[:, i * 128:(i + 1) * 128] = gain_in[i * 128:(i + 1) * 128].reshape(1, 128)

    def norm_step(i, _):
        rows = pl.ds(pl.multiple_of(i * 16, 16), 16)
        h = hid[rows, :].astype(F32)
        inv = lax.rsqrt(jnp.mean(h * h, axis=1, keepdims=True) + epsilon)
        norm_all[0, rows, :] = (h * inv * gain[...]).astype(BF16)
        return 0

    lax.fori_loop(0, ROWS // 16, norm_step, 0)
    n_r = send(norm_all.at[0], norm_all.at[2], right)
    n_l = send(norm_all.at[0], norm_all.at[1], left)
    for i in range(32):
        gain_t[i:i + 1, 0:PR] = gain[:, i * PR:(i + 1) * PR]

    for s in range(1, 4):
        ups[-1].wait_recv()
        ups.append(send(pblock(zp(8 - s)), pblock(zp(8 - s)), above))
        dns[-1].wait_recv()
        if s < 3:
            dns.append(send(pblock(zp(s)), pblock(zp(s)), below))
        if s == 2:
            z_msgs.append(raw(1 - zl, 2, 0, z_in.at[0], pair))
    arrived(*x_fwd_r)
    for copy in load_ma:
        copy.wait()
    merge(t_ma, (t_ma, x_fl), 4)
    x_last = [send(t_ma, x_gl.at[0], right)]
    arrived(*x_fwd_l)
    for copy in load_mb:
        copy.wait()
    merge(t_mb, (t_mb, x_fr), 4)
    x_last += [send(t_mb, x_gr.at[1], left)]
    x_last += raw(1, 1, 1, x_gl.at[1], right)
    x_last += raw(0, 3, 1, x_gr.at[0], left)
    z_msgs.append(raw(1 - zl, 1, 0, z_in.at[1], pair))
    ups[-1].wait_recv()
    own.wait()
    y_up = send(proj_full.at[y, :, c], proj_full.at[y, :, c], up)
    y_dn = send(proj_full.at[y, :, c], proj_full.at[y, :, c], down)
    core = [send(proj_full.at[y, :, c], proj_full.at[y, :, c], mate)]
    z_msgs.append(raw(1 - zl, 3, 0, z_in.at[2], pair))

    transpose(0)
    a, b = pl.ds(0, 2), pl.ds(2, 2)

    def z_merge(k):
        arrived(*z_msgs[k])
        for copy in load_z[k]:
            copy.wait()
        merge(t_z.at[k], (t_z.at[k], z_in.at[k]), 4)

    z_merge(0)
    z_msgs.append(raw(1 - zl, 0, 0, z_in.at[3], pair))

    y_up.wait_recv()
    y_up2 = send(proj_full.at[yp(3), a, c], proj_full.at[yp(3), a, c], up)
    core.append(send(proj_full.at[yp(3), :, c], proj_full.at[yp(3), :, c], mate))
    y_dn.wait_recv()
    y_dn2 = send(proj_full.at[yp(1), b, c], proj_full.at[yp(1), b, c], down)
    core.append(send(proj_full.at[yp(1), :, c], proj_full.at[yp(1), :, c], mate))

    lo, hi = pl.ds(0, ROWS // 2), pl.ds(ROWS // 2, ROWS // 2)
    n_r.wait_recv()
    n_r2 = send(norm_all.at[2, lo], norm_all.at[3, lo], right)
    n_l.wait_recv()
    n_l2 = send(norm_all.at[1, hi], norm_all.at[3, hi], left)
    transpose(1)
    transpose(2)
    z_merge(1)
    z_merge(2)
    arrived(*x_last)
    for copy in load_own:
        copy.wait()
    for t in range(2):
        merge(x_sum.at[t], (t_own.at[t], x_gl.at[t], x_gr.at[t]), 4)
    z_msg2 = send(x_sum.at[1 - zl], z_in2, pair)
    s_fwd_r = send(t_z.at[0, a], s_fl, right)
    s_fwd_l = send(t_z.at[0, b], s_fr, left)


    y_up2.wait_recv()
    y_dn2.wait_recv()
    core.append(send(proj_full.at[yp(2), :, c], proj_full.at[yp(2), :, c], mate))
    arrived(*core)
    pred_part(1, 0, 3)
    pred_part(0, 0, 3)
    arrived(n_r2, n_l2)

    s_last = [send(t_z.at[1, b], s_gl.at[b], right)]
    s_last += [send(t_z.at[2, a], s_gr.at[a], left)]

    transpose(3)
    pred_part(1, 3, 4)
    pred_part(0, 3, 4)

    def mismatch_part(part, terms):
        cols = slice(part * PC, part * PC + PC)

        total = jnp.zeros((1, PC), F32)
        for p in range(4):
            t = xp(places[p])

            def step(i, loss):
                rows = pl.ds(pl.multiple_of(i * 16, 16), 16)
                out_rows = pl.ds(pl.multiple_of(p * ROWS + i * 16, 16), 16)
                target = terms[0][t, rows, :].astype(F32)
                for term in terms[1:]:
                    target = target + term[t, rows, :].astype(F32)
                miss = pred[out_rows, cols].astype(F32) - target
                pgrad[out_rows, cols] = miss.astype(BF16)
                return loss + jnp.sum(miss * miss, axis=0, keepdims=True)

            total = lax.fori_loop(0, ROWS // 16, step, total)
        return total

    def ngrad_half(part, k):
        def step(i, _):
            yy = 2 * k + i
            cols = pl.ds(pl.multiple_of(yy * YR, 128), YR)
            total = jnp.zeros((4 * ROWS, YR), F32)
            for m in range(2):
                weights = proj_full[yy, :, :, :, m * PC + part * HP:m * PC + part * HP + HP]
                total = total + lax.dot_general(
                    pgrad[:, part * PC + m * HP:part * PC + m * HP + HP],
                    weights.reshape(YR, HP), (((1,), (1,)), ((), ())),
                    preferred_element_type=F32)
            total = total.reshape(4, ROWS, YR)
            if part == 0:
                total = total + ng[:, :, cols].astype(F32)
            ng[:, :, cols] = total.astype(BF16)
            return 0

        lax.fori_loop(0, 2, step, 0)

    y2, y1, y3 = yp(2), yp(1), yp(3)

    def pgrad_block(q, yy):
        rows = pl.ds(pl.multiple_of(yy * YR, 128), YR)
        product = jnp.dot(norm_t[rows, :], pgrad[:, q * PC:q * PC + PC], preferred_element_type=F32)
        pg[q, yy] = product.astype(BF16).reshape(4, 2, PR, PC)
        return send(pg.at[q, yy, :, 1 - c], c_in.at[q, yy], mate)

    def core_merge(q, copy, yy):
        copy.wait_recv()
        merge(c_in.at[q, yy], (c_in.at[q, yy], pg.at[q, yy, :, c]), 4)

    def pgrad_sends(q):
        c_2 = pgrad_block(q, y2)
        c_1 = pgrad_block(q, y1)
        c_3 = pgrad_block(q, y3)
        c_0 = pgrad_block(q, y)
        core_merge(q, c_2, y2)
        fwd_u = send(c_in.at[q, y2, a], y_fl.at[q], up)
        fwd_d = send(c_in.at[q, y2, b], y_fr.at[q], down)
        core_merge(q, c_1, y1)
        dir_u = send(c_in.at[q, y1, b], y_gl.at[q, b], up)
        core_merge(q, c_3, y3)
        dir_d = send(c_in.at[q, y3, a], y_gr.at[q, a], down)
        core_merge(q, c_0, y)
        return fwd_u, fwd_d, dir_u, dir_d

    def y_merge(q, fwd_u, fwd_d, dir_u, dir_d):
        fwd_u.wait_recv()
        merge(c_in.at[q, y1, a], (c_in.at[q, y1, a], y_fl.at[q]), 2)
        mrg_u = send(c_in.at[q, y1, a], y_gl.at[q, a], up)
        fwd_d.wait_recv()
        merge(c_in.at[q, y3, b], (c_in.at[q, y3, b], y_fr.at[q]), 2)
        mrg_d = send(c_in.at[q, y3, b], y_gr.at[q, b], down)
        return dir_u, dir_d, mrg_u, mrg_d

    def sblock(q, d):
        zz = zp(d)
        return y_sum.at[q, zz // 2, :, pl.ds(pl.multiple_of((zz % 2) * HP, HP), HP)]

    def z_sends(q, copies):
        arrived(*copies)
        merge(y_sum.at[q], (c_in.at[q, y], y_gl.at[q], y_gr.at[q]), 4)
        return [send(sblock(q, d), zd_in.at[q, d - 1], device(z=zp(d)))
                for d in (4, 3, 5, 2, 6, 1, 7)]

    s_fwd_r.wait_recv()
    merge(t_z.at[1, a], (t_z.at[1, a], s_fl), 2)
    s_last += [send(t_z.at[1, a], s_gl.at[a], right)]
    s_fwd_l.wait_recv()
    merge(t_z.at[2, b], (t_z.at[2, b], s_fr), 2)
    s_last += [send(t_z.at[2, b], s_gr.at[b], left)]
    z_msg2.wait_recv()
    loss = mismatch_part(1, (x_sum.at[zl], z_in2))
    y_1 = pgrad_sends(1)
    ngrad_half(1, 0)
    ngrad_half(1, 1)
    y_1 = y_merge(1, *y_1)

    arrived(*z_msgs[3])
    for copy in load_z[3]:
        copy.wait()
    arrived(*s_last)
    loss = loss + mismatch_part(0, (t_z.at[3], z_in.at[3], s_gl, s_gr))
    loss = jnp.sum(loss, axis=1, keepdims=True)
    ca, cb = pl.ds(0, HALF), pl.ds(HALF, HALF)
    y_0 = pgrad_sends(0)
    ngrad_half(0, 0)
    n_fwd_r = send(ng.at[3, :, ca], n_fl, right)
    n_last = [send(ng.at[2, :, ca], n_gr.at[:, ca], left)]
    ngrad_half(0, 1)
    n_fwd_l = send(ng.at[3, :, cb], n_fr, left)
    n_last += [send(ng.at[1, :, cb], n_gl.at[:, cb], right)]
    y_0 = y_merge(0, *y_0)
    z_1 = z_sends(1, y_1)
    n_fwd_r.wait_recv()
    merge_rows(ng.at[1, :, ca], (ng.at[1, :, ca], n_fl), ROWS)
    n_last += [send(ng.at[1, :, ca], n_gl.at[:, ca], right)]
    z_0 = z_sends(0, y_0)
    n_fwd_l.wait_recv()
    merge_rows(ng.at[2, :, cb], (ng.at[2, :, cb], n_fr), ROWS)
    n_last += [send(ng.at[2, :, cb], n_gr.at[:, cb], left)]
    squares = jnp.zeros((PR, HP), F32)
    gains = jnp.zeros((PR, HP), F32)
    for q, copies in ((1, z_1), (0, z_0)):
        arrived(*copies)
        block = sblock(q, 0)[...].astype(F32)
        for d in range(7):
            block = block + zd_in[q, d].astype(F32)
        cols = slice(q * HP, q * HP + HP)
        proj_out[:, cols] = block
        squares = squares + block * block
        gains = gains + block * proj[:, cols].astype(F32)
    squares = jnp.sum(jnp.sum(squares, axis=0, keepdims=True), axis=1, keepdims=True)
    gains = gains[:, :128] + gains[:, 128:]
    gains = jnp.concatenate([gains, jnp.zeros((128 - PR, 128), F32)], axis=0)
    gains = jnp.sum(gains.T, axis=0, keepdims=True)

    row = lax.broadcasted_iota(jnp.int32, (8, 128), 0)
    pack = jnp.where(row == 0, gains, jnp.where(row == 1, squares, jnp.where(row == 2, loss, 0.0)))
    m_1[...] = pack
    s_1[c * 8 + z] = pack
    small = [send(m_1, s_1.at[c * 8 + z], dev) for dev in peers_1]
    arrived(*small)
    total = s_1[0]
    for i in range(1, 16):
        total = total + s_1[i]
    for i in range(4):
        for k in range(2):
            m_2[i * 2 + k:i * 2 + k + 1, :] = s_1[k * 8 + 2 * i, 0:1, :] + s_1[k * 8 + 2 * i + 1, 0:1, :]
    m_2[8:16, :] = total
    s_2[x * 4 + y] = m_2[...]
    small = [send(m_2, s_2.at[x * 4 + y], dev) for dev in peers_2]

    arrived(*n_last)

    def hid_step(i, _):
        rows = pl.ds(pl.multiple_of(i * 16, 16), 16)
        g = ng[0, rows, :].astype(F32) + n_gl[rows, :].astype(F32) + n_gr[rows, :].astype(F32)
        h = hid[rows, :].astype(F32)
        inv = lax.rsqrt(jnp.mean(h * h, axis=1, keepdims=True) + epsilon)
        scaled = h * inv
        g = g * gain[...]
        mean = jnp.mean(g * scaled, axis=1, keepdims=True)
        hid_out[rows, :] = (inv * (g - scaled * mean)).astype(BF16)
        return 0

    lax.fori_loop(0, ROWS // 16, hid_step, 0)

    arrived(*small)
    total = s_2[0, 8:16, :]
    for i in range(1, 16):
        total = total + s_2[i, 8:16, :]
    gain_grads = []
    gain_squares = jnp.zeros((1, 1), F32)
    for k in range(4):
        block = s_2[k, 0:8, :] + s_2[4 + k, 0:8, :] + s_2[8 + k, 0:8, :] + s_2[12 + k, 0:8, :]
        block = block[:, 0:PR] / gain_t[8 * k:8 * k + 8, 0:PR]
        gain_grads.append(block)
        gain_squares = gain_squares + jnp.sum(
            jnp.sum(block * block, axis=0, keepdims=True), axis=1, keepdims=True)
    factor = lax.rsqrt((total[1:2, 0:1] + gain_squares) / (DS * DT + DS) + epsilon)
    proj_out[...] = proj_out[...] * factor
    for k in range(4):
        gain_out[8 * k:8 * k + 8, :] = gain_grads[k] * factor
    loss_out[...] = total[2:3, :] / (32768 * DT)

    for copy in opened:
        copy.wait_send()


def finish(loss, hid, proj, gain, loss_out, hid_out, proj_out, gain_out, row, block, sem):
    parts = [pl.ds(i * 32, 32) for i in range(4)]
    loads = [pltpu.make_async_copy(hid.at[p], block.at[p], sem.at[i]) for i, p in enumerate(parts)]
    for copy in loads:
        copy.start()
    proj_out[...] = proj[...]
    loss_out[...] = loss[...]
    for i in range(32):
        row[:, i * PR:(i + 1) * PR] = gain[i:i + 1, :]
    for i in range(DS // 128):
        gain_out[i * 128:(i + 1) * 128] = row[0, i * 128:(i + 1) * 128]
    stores = []
    for i, p in enumerate(parts):
        loads[i].wait()
        stores.append(pltpu.make_async_copy(block.at[p], hid_out.at[p], sem.at[4 + i]))
        stores[i].start()
    for copy in stores:
        copy.wait()


def shards(student_hidden, norm_gain, projection, teacher_terms):
    teach = teacher_terms.reshape(4, 2, ROWS, DT)
    vmem = pl.BlockSpec(memory_space=pltpu.VMEM)
    V = pltpu.VMEM
    loss, hidden_grad, projection_update, gain_update = pl.pallas_call(
        kernel,
        out_shape=(
            jax.ShapeDtypeStruct((1, 128), F32),
            jax.ShapeDtypeStruct((ROWS, DS), BF16),
            jax.ShapeDtypeStruct((PR, PC), F32),
            jax.ShapeDtypeStruct((32, PR), F32),
        ),
        in_specs=[vmem, vmem, vmem, pl.BlockSpec(memory_space=pl.ANY)],
        out_specs=(vmem,) * 4,
        scratch_shapes=[
            V((4, ROWS, DS), BF16), V((DS, 4 * ROWS), BF16), V((4, 4, 2, PR, FX), BF16),
            V((4, ROWS, PC), BF16), V((4, ROWS, PC), BF16), V((2, 4, ROWS, PC), BF16),
            V((4, 4, ROWS, PC), BF16),
            V((4, 4, ROWS, PC), BF16),
            V((4, ROWS, PC), BF16), V((4, ROWS, PC), BF16),
            V((2, 4, ROWS, PC), BF16), V((2, 4, ROWS, PC), BF16), V((2, 4, ROWS, PC), BF16),
            V((4, ROWS, PC), BF16),
            V((2, ROWS, PC), BF16), V((2, ROWS, PC), BF16),
            V((4, ROWS, PC), BF16), V((4, ROWS, PC), BF16),
            V((4 * ROWS, FX), BF16), V((4 * ROWS, FX), BF16),
            V((2, 4, 4, 2, PR, PC), BF16), V((2, 4, 4, PR, PC), BF16),
            V((2, 2, PR, PC), BF16), V((2, 2, PR, PC), BF16),
            V((2, 4, PR, PC), BF16), V((2, 4, PR, PC), BF16), V((2, 4, PR, PC), BF16),
            V((2, 7, PR, HP), BF16),
            V((4, ROWS, DS), BF16), V((ROWS, HALF), BF16), V((ROWS, HALF), BF16),
            V((ROWS, DS), BF16), V((ROWS, DS), BF16),
            V((1, DS), F32), V((32, 128), F32), V((8, 128), F32), V((16, 128), F32),
            V((16, 8, 128), F32), V((16, 16, 128), F32),
            pltpu.SemaphoreType.DMA((N_MSG,)), pltpu.SemaphoreType.DMA((N_MSG,)),
            pltpu.SemaphoreType.DMA((24,)),
        ],
        compiler_params=pltpu.CompilerParams(
            collective_id=0, has_side_effects=True, vmem_limit_bytes=62 * 1024 * 1024
        ),
    )(student_hidden, norm_gain, projection, teach)
    loss, hidden_grad, projection_update, gain_update = pl.pallas_call(
        finish,
        out_shape=(
            jax.ShapeDtypeStruct((1, 128), F32),
            jax.ShapeDtypeStruct((ROWS, DS), BF16),
            jax.ShapeDtypeStruct((PR, PC), F32),
            jax.ShapeDtypeStruct((DS,), F32),
        ),
        in_specs=[vmem, pl.BlockSpec(memory_space=pl.ANY), vmem, vmem],
        out_specs=(vmem, pl.BlockSpec(memory_space=pl.ANY), vmem, vmem),
        scratch_shapes=[V((1, DS), F32), V((ROWS, DS), BF16), pltpu.SemaphoreType.DMA((8,))],
        compiler_params=pltpu.CompilerParams(vmem_limit_bytes=62 * 1024 * 1024),
    )(loss, hidden_grad, projection_update, gain_update)
    return loss[0, 0], hidden_grad, projection_update, gain_update


def solution(mesh):
    in_specs = (P(("dp", "tensor"), None), P(), P("dp", "tensor"), P("tensor", "dp", None))
    out_specs = (P(), P(("dp", "tensor"), None), P("dp", "tensor"), P())
    return jax.shard_map(shards, mesh=mesh, in_specs=in_specs, out_specs=out_specs, check_vma=False)
```

```python
import jax
import jax.numpy as jnp
from jax import lax
from jax.experimental import pallas as pl
from jax.experimental.pallas import tpu as pltpu
from jax.sharding import PartitionSpec as P

epsilon = 1e-06
MESH = pl.DeviceIdType.MESH
F32 = jnp.float32
BF16 = jnp.bfloat16

ROWS = 128
DS = 3584
PR = 112
PC = 512
DT = 4096
FX = 1024
HP = 256
HALF = DS // 2
YR = DS // 4
N_MSG = 160


def kernel(
    hid, gain_in, proj, teach,
    loss_out, hid_out, proj_out, gain_out,
    norm_all, norm_t, proj_full,
    t_ma, t_mb, t_own, t_z,
    z_in, x_fl, x_fr, x_gl, x_gr, x_sum, z_in2, s_fl, s_fr, s_gl, s_gr,
    pred, pgrad,
    pg, c_in, y_fl, y_fr, y_gl, y_gr, y_sum, zd_in, zf_in,
    ng, n_fl, n_fr, n_gl, n_gr,
    gain, gain_t, m_1, m_2, s_1, s_2,
    send_sem, recv_sem, local_sem,
):
    dp = lax.axis_index("dp")
    tp = lax.axis_index("tensor")
    y, zh, c = dp // 8, (dp // 2) % 4, dp % 2
    x, zl = tp // 2, tp % 2
    z = zh * 2 + zl

    def device(y=y, z=z, c=c, x=x):
        return ((y * 4 + z // 2) * 2 + c, x * 2 + z % 2)

    def xp(d):
        return (x + d) % 4

    def yp(d):
        return (y + d) % 4

    def zp(d):
        return (z + d) % 8

    right, left = device(x=xp(1)), device(x=xp(3))
    up, down = device(y=yp(1)), device(y=yp(3))
    above, below = device(z=zp(1)), device(z=zp(7))
    mate = device(c=1 - c)
    pair = device(z=z + 1 - 2 * zl)

    opened = []

    def send(src, dst, dev):
        i = len(opened)
        copy = pltpu.make_async_remote_copy(
            src_ref=src, dst_ref=dst, send_sem=send_sem.at[i], recv_sem=recv_sem.at[i],
            device_id=dev, device_id_type=MESH,
        )
        copy.start()
        opened.append(copy)
        return copy

    n_local = [0]

    def fetch(src, dst):
        copy = pltpu.make_async_copy(src, dst, local_sem.at[n_local[0]])
        n_local[0] += 1
        copy.start()
        return copy

    def arrived(*copies):
        for copy in copies:
            copy.wait_recv()

    def merge(out, parts, n):
        def step(i, _):
            total = parts[0][i].astype(F32)
            for part in parts[1:]:
                total = total + part[i].astype(F32)
            out[i] = total.astype(out.dtype)
            return 0
        lax.fori_loop(0, n, step, 0)

    def merge_rows(out, parts, n):
        def step(i, _):
            rows = pl.ds(pl.multiple_of(i * 16, 16), 16)
            total = parts[0][rows, :].astype(F32)
            for part in parts[1:]:
                total = total + part[rows, :].astype(F32)
            out[rows, :] = total.astype(out.dtype)
            return 0
        lax.fori_loop(0, n // 16, step, 0)

    def transpose(t):
        out_cols = slice(t * ROWS, t * ROWS + ROWS)

        def step(i, _):
            cols = pl.ds(pl.multiple_of(i * 512, 512), 512)
            norm_t[cols, out_cols] = norm_all[t, :, cols].T
            return 0

        lax.fori_loop(0, DS // 512, step, 0)

    places = (0, 1, 3, 2)

    def pred_part(part, first, end):
        rows = slice(first * ROWS, end * ROWS)

        def step(k, _):
            cols = pl.ds(pl.multiple_of(k * PC + part * HP, HP), HP)
            out_cols = pl.ds(pl.multiple_of(part * PC + k * HP, HP), HP)
            rows_part = norm_all[first:end].reshape((end - first) * ROWS, DS)
            cols_part = proj_full[:, :, :, :, cols].reshape(DS, HP)
            product = jnp.dot(rows_part, cols_part, preferred_element_type=F32)
            pred[rows, out_cols] = product.astype(BF16)
            return 0

        lax.fori_loop(0, 2, step, 0)

    group_1 = [(dc, dz) for dc in range(2) for dz in range(8) if dc or dz]
    group_2 = [(dx, dy) for dx in range(4) for dy in range(4) if dx or dy]
    peers_1 = [device(c=(c + dc) % 2, z=zp(dz)) for dc, dz in group_1]
    peers_2 = [device(x=xp(dx), y=yp(dy)) for dx, dy in group_2]
    barrier = pltpu.get_barrier_semaphore()
    for dev in peers_1 + peers_2:
        pl.semaphore_signal(barrier, inc=1, device_id=dev, device_id_type=MESH)
    pl.semaphore_wait(barrier, len(peers_1) + len(peers_2))

    def tcols(d, part, k):
        return pl.ds(pl.multiple_of(xp(d) * FX + k * PC + part * HP, HP), HP)

    def raw(t, d, part, dst, dev):
        return [send(teach.at[:, t, :, tcols(d, part, k)], dst.at[:, :, pl.ds(k * HP, HP)], dev)
                for k in range(2)]

    def load(t, d, part, dst):
        return [fetch(teach.at[:, t, :, tcols(d, part, k)], dst.at[:, :, pl.ds(k * HP, HP)])
                for k in range(2)]

    def pblock(zz):
        return proj_full.at[y, zz // 2, c, :, pl.ds(pl.multiple_of((zz % 2) * PC, PC), PC)]

    ups = [send(proj, pblock(z), above)]
    dns = [send(proj, pblock(z), below)]
    x_fwd_r = raw(0, 2, 1, x_fl, right)
    x_fwd_l = raw(1, 2, 1, x_fr, left)
    order = (2, 1, 3, 0)
    z_msgs = []
    own = fetch(proj, pblock(z))
    load_ma = load(0, 1, 1, t_ma)
    load_mb = load(1, 3, 1, t_mb)
    load_z = [load(zl, d, 0, t_z.at[k]) for k, d in enumerate(order)]
    load_own = load(0, 0, 1, t_own.at[0]) + load(1, 0, 1, t_own.at[1])

    for i in range(DS // 128):
        gain[:, i * 128:(i + 1) * 128] = gain_in[i * 128:(i + 1) * 128].reshape(1, 128)

    def norm_step(i, _):
        rows = pl.ds(pl.multiple_of(i * 16, 16), 16)
        h = hid[rows, :].astype(F32)
        inv = lax.rsqrt(jnp.mean(h * h, axis=1, keepdims=True) + epsilon)
        norm_all[0, rows, :] = (h * inv * gain[...]).astype(BF16)
        return 0

    lax.fori_loop(0, ROWS // 16, norm_step, 0)
    n_r = send(norm_all.at[0], norm_all.at[2], right)
    n_l = send(norm_all.at[0], norm_all.at[1], left)
    for i in range(32):
        gain_t[i:i + 1, 0:PR] = gain[:, i * PR:(i + 1) * PR]

    for s in range(1, 4):
        ups[-1].wait_recv()
        ups.append(send(pblock(zp(8 - s)), pblock(zp(8 - s)), above))
        dns[-1].wait_recv()
        if s < 3:
            dns.append(send(pblock(zp(s)), pblock(zp(s)), below))
        if s == 2:
            z_msgs.append(raw(1 - zl, 2, 0, z_in.at[0], pair))
    arrived(*x_fwd_r)
    for copy in load_ma:
        copy.wait()
    merge(t_ma, (t_ma, x_fl), 4)
    x_last = [send(t_ma, x_gl.at[0], right)]
    arrived(*x_fwd_l)
    for copy in load_mb:
        copy.wait()
    merge(t_mb, (t_mb, x_fr), 4)
    x_last += [send(t_mb, x_gr.at[1], left)]
    x_last += raw(1, 1, 1, x_gl.at[1], right)
    x_last += raw(0, 3, 1, x_gr.at[0], left)
    z_msgs.append(raw(1 - zl, 1, 0, z_in.at[1], pair))
    ups[-1].wait_recv()
    own.wait()
    y_up = send(proj_full.at[y, :, c], proj_full.at[y, :, c], up)
    y_dn = send(proj_full.at[y, :, c], proj_full.at[y, :, c], down)
    core = [send(proj_full.at[y, :, c], proj_full.at[y, :, c], mate)]
    z_msgs.append(raw(1 - zl, 3, 0, z_in.at[2], pair))

    transpose(0)
    a, b = pl.ds(0, 2), pl.ds(2, 2)

    def z_merge(k):
        arrived(*z_msgs[k])
        for copy in load_z[k]:
            copy.wait()
        merge(t_z.at[k], (t_z.at[k], z_in.at[k]), 4)

    z_merge(0)
    z_msgs.append(raw(1 - zl, 0, 0, z_in.at[3], pair))

    y_up.wait_recv()
    y_up2 = send(proj_full.at[yp(3), a, c], proj_full.at[yp(3), a, c], up)
    core.append(send(proj_full.at[yp(3), :, c], proj_full.at[yp(3), :, c], mate))
    y_dn.wait_recv()
    y_dn2 = send(proj_full.at[yp(1), b, c], proj_full.at[yp(1), b, c], down)
    core.append(send(proj_full.at[yp(1), :, c], proj_full.at[yp(1), :, c], mate))

    lo, hi = pl.ds(0, ROWS // 2), pl.ds(ROWS // 2, ROWS // 2)
    n_r.wait_recv()
    n_r2 = send(norm_all.at[2, lo], norm_all.at[3, lo], right)
    n_l.wait_recv()
    n_l2 = send(norm_all.at[1, hi], norm_all.at[3, hi], left)
    transpose(1)
    transpose(2)
    z_merge(1)
    z_merge(2)
    arrived(*x_last)
    for copy in load_own:
        copy.wait()
    other = 1 - zl
    merge(x_sum.at[other], (t_own.at[other], x_gl.at[other], x_gr.at[other]), 4)
    z_msg2 = send(x_sum.at[other], z_in2, pair)
    merge(x_sum.at[zl], (t_own.at[zl], x_gl.at[zl], x_gr.at[zl]), 4)
    s_fwd_r = send(t_z.at[0, a], s_fl, right)
    s_fwd_l = send(t_z.at[0, b], s_fr, left)


    y_up2.wait_recv()
    y_dn2.wait_recv()
    core.append(send(proj_full.at[yp(2), :, c], proj_full.at[yp(2), :, c], mate))
    arrived(*core)
    pred_part(1, 0, 3)
    pred_part(0, 0, 3)
    arrived(n_r2, n_l2)

    s_last = [send(t_z.at[1, b], s_gl.at[b], right)]
    s_last += [send(t_z.at[2, a], s_gr.at[a], left)]

    transpose(3)
    pred_part(1, 3, 4)

    def mismatch_part(part, terms):
        cols = slice(part * PC, part * PC + PC)

        total = jnp.zeros((1, PC), F32)
        for p in range(4):
            t = xp(places[p])

            def step(i, loss):
                rows = pl.ds(pl.multiple_of(i * 16, 16), 16)
                out_rows = pl.ds(pl.multiple_of(p * ROWS + i * 16, 16), 16)
                target = terms[0][t, rows, :].astype(F32)
                for term in terms[1:]:
                    target = target + term[t, rows, :].astype(F32)
                miss = pred[out_rows, cols].astype(F32) - target
                pgrad[out_rows, cols] = miss.astype(BF16)
                return loss + jnp.sum(miss * miss, axis=0, keepdims=True)

            total = lax.fori_loop(0, ROWS // 16, step, total)
        return total

    def ngrad_half(part, k):
        def step(i, _):
            yy = 2 * k + i
            cols = pl.ds(pl.multiple_of(yy * YR, 128), YR)
            total = jnp.zeros((4 * ROWS, YR), F32)
            for m in range(2):
                weights = proj_full[yy, :, :, :, m * PC + part * HP:m * PC + part * HP + HP]
                total = total + lax.dot_general(
                    pgrad[:, part * PC + m * HP:part * PC + m * HP + HP],
                    weights.reshape(YR, HP), (((1,), (1,)), ((), ())),
                    preferred_element_type=F32)
            total = total.reshape(4, ROWS, YR)
            if part == 0:
                total = total + ng[:, :, cols].astype(F32)
            ng[:, :, cols] = total.astype(BF16)
            return 0

        lax.fori_loop(0, 2, step, 0)

    y2, y1, y3 = yp(2), yp(1), yp(3)

    def pgrad_block(q, yy):
        rows = pl.ds(pl.multiple_of(yy * YR, 128), YR)
        product = jnp.dot(norm_t[rows, :], pgrad[:, q * PC:q * PC + PC], preferred_element_type=F32)
        pg[q, yy] = product.astype(BF16).reshape(4, 2, PR, PC)
        return send(pg.at[q, yy, :, 1 - c], c_in.at[q, yy], mate)

    def core_merge(q, copy, yy):
        copy.wait_recv()
        merge(c_in.at[q, yy], (c_in.at[q, yy], pg.at[q, yy, :, c]), 4)

    def pgrad_begin(q):
        return pgrad_block(q, y2), pgrad_block(q, y1)

    def pgrad_sends(q, c_2, c_1):
        core_merge(q, c_2, y2)
        fwd_u = send(c_in.at[q, y2, a], y_fl.at[q], up)
        fwd_d = send(c_in.at[q, y2, b], y_fr.at[q], down)
        c_3 = pgrad_block(q, y3)
        core_merge(q, c_1, y1)
        dir_u = send(c_in.at[q, y1, b], y_gl.at[q, b], up)
        c_0 = pgrad_block(q, y)
        core_merge(q, c_3, y3)
        dir_d = send(c_in.at[q, y3, a], y_gr.at[q, a], down)
        return (fwd_u, fwd_d, dir_u, dir_d), c_0

    def y_merge(q, fwd_u, fwd_d, dir_u, dir_d):
        fwd_u.wait_recv()
        merge(c_in.at[q, y1, a], (c_in.at[q, y1, a], y_fl.at[q]), 2)
        mrg_u = send(c_in.at[q, y1, a], y_gl.at[q, a], up)
        fwd_d.wait_recv()
        merge(c_in.at[q, y3, b], (c_in.at[q, y3, b], y_fr.at[q]), 2)
        mrg_d = send(c_in.at[q, y3, b], y_gr.at[q, b], down)
        return dir_u, dir_d, mrg_u, mrg_d

    def sblock(q, d):
        zz = zp(d)
        return y_sum.at[q, zz // 2, :, pl.ds(pl.multiple_of((zz % 2) * HP, HP), HP)]

    def z_sends(q, copies):
        arrived(*copies)
        merge(y_sum.at[q], (c_in.at[q, y], y_gl.at[q], y_gr.at[q]), 4)
        far = send(sblock(q, 4), zf_in.at[q], below)
        near = [send(sblock(q, d), zd_in.at[q, d - 1], device(z=zp(d))) for d in (3, 2, 6, 1, 7)]
        return far, near

    def z_finish(q, far, near):
        far.wait_recv()
        block = sblock(q, 5)
        block[...] = (block[...].astype(F32) + zf_in[q].astype(F32)).astype(BF16)
        return near + [send(block, zd_in.at[q, 4], device(z=zp(5)))]

    z_msg2.wait_recv()
    loss = mismatch_part(1, (x_sum.at[zl], z_in2))
    begun = pgrad_begin(1)
    pred_part(0, 3, 4)
    s_fwd_r.wait_recv()
    merge(t_z.at[1, a], (t_z.at[1, a], s_fl), 2)
    s_last += [send(t_z.at[1, a], s_gl.at[a], right)]
    s_fwd_l.wait_recv()
    merge(t_z.at[2, b], (t_z.at[2, b], s_fr), 2)
    s_last += [send(t_z.at[2, b], s_gr.at[b], left)]
    y_1, own_1 = pgrad_sends(1, *begun)
    ngrad_half(1, 0)
    ngrad_half(1, 1)
    core_merge(1, own_1, y)

    arrived(*z_msgs[3])
    for copy in load_z[3]:
        copy.wait()
    arrived(*s_last)
    loss = loss + mismatch_part(0, (t_z.at[3], z_in.at[3], s_gl, s_gr))
    loss = jnp.sum(loss, axis=1, keepdims=True)
    ca, cb = pl.ds(0, HALF), pl.ds(HALF, HALF)
    begun = pgrad_begin(0)
    y_1 = y_merge(1, *y_1)
    y_0, own_0 = pgrad_sends(0, *begun)
    ngrad_half(0, 0)
    n_fwd_r = send(ng.at[3, :, ca], n_fl, right)
    n_last = [send(ng.at[2, :, ca], n_gr.at[:, ca], left)]
    ngrad_half(0, 1)
    n_fwd_l = send(ng.at[3, :, cb], n_fr, left)
    n_last += [send(ng.at[1, :, cb], n_gl.at[:, cb], right)]
    core_merge(0, own_0, y)
    z_1 = z_sends(1, y_1)
    y_0 = y_merge(0, *y_0)
    z_1 = z_finish(1, *z_1)
    n_fwd_r.wait_recv()
    merge_rows(ng.at[1, :, ca], (ng.at[1, :, ca], n_fl), ROWS)
    n_last += [send(ng.at[1, :, ca], n_gl.at[:, ca], right)]
    z_0 = z_sends(0, y_0)
    n_fwd_l.wait_recv()
    merge_rows(ng.at[2, :, cb], (ng.at[2, :, cb], n_fr), ROWS)
    n_last += [send(ng.at[2, :, cb], n_gr.at[:, cb], left)]
    z_0 = z_finish(0, *z_0)

    squares = jnp.zeros((PR, HP), F32)
    gains = jnp.zeros((PR, HP), F32)
    for q, copies in ((1, z_1), (0, z_0)):
        arrived(*copies)
        block = sblock(q, 0)[...].astype(F32)
        for d in (0, 1, 2, 4, 5, 6):
            block = block + zd_in[q, d].astype(F32)
        cols = slice(q * HP, q * HP + HP)
        proj_out[:, cols] = block
        squares = squares + block * block
        gains = gains + block * proj[:, cols].astype(F32)
    squares = jnp.sum(jnp.sum(squares, axis=0, keepdims=True), axis=1, keepdims=True)
    gains = gains[:, :128] + gains[:, 128:]
    gains = jnp.concatenate([gains, jnp.zeros((128 - PR, 128), F32)], axis=0)
    gains = jnp.sum(gains.T, axis=0, keepdims=True)

    row = lax.broadcasted_iota(jnp.int32, (8, 128), 0)
    pack = jnp.where(row == 0, gains, jnp.where(row == 1, squares, jnp.where(row == 2, loss, 0.0)))
    m_1[...] = pack
    s_1[c * 8 + z] = pack
    small = [send(m_1, s_1.at[c * 8 + z], dev) for dev in peers_1]
    arrived(*small)
    total = s_1[0]
    for i in range(1, 16):
        total = total + s_1[i]
    for i in range(4):
        for k in range(2):
            m_2[i * 2 + k:i * 2 + k + 1, :] = s_1[k * 8 + 2 * i, 0:1, :] + s_1[k * 8 + 2 * i + 1, 0:1, :]
    m_2[8:16, :] = total
    s_2[x * 4 + y] = m_2[...]
    small = [send(m_2, s_2.at[x * 4 + y], dev) for dev in peers_2]

    arrived(*n_last)

    def hid_step(i, _):
        rows = pl.ds(pl.multiple_of(i * 16, 16), 16)
        g = ng[0, rows, :].astype(F32) + n_gl[rows, :].astype(F32) + n_gr[rows, :].astype(F32)
        h = hid[rows, :].astype(F32)
        inv = lax.rsqrt(jnp.mean(h * h, axis=1, keepdims=True) + epsilon)
        scaled = h * inv
        g = g * gain[...]
        mean = jnp.mean(g * scaled, axis=1, keepdims=True)
        hid_out[rows, :] = (inv * (g - scaled * mean)).astype(BF16)
        return 0

    lax.fori_loop(0, ROWS // 16, hid_step, 0)

    arrived(*small)
    total = s_2[0, 8:16, :]
    for i in range(1, 16):
        total = total + s_2[i, 8:16, :]
    gain_grads = []
    gain_squares = jnp.zeros((1, 1), F32)
    for k in range(4):
        block = s_2[k, 0:8, :] + s_2[4 + k, 0:8, :] + s_2[8 + k, 0:8, :] + s_2[12 + k, 0:8, :]
        block = block[:, 0:PR] / gain_t[8 * k:8 * k + 8, 0:PR]
        gain_grads.append(block)
        gain_squares = gain_squares + jnp.sum(
            jnp.sum(block * block, axis=0, keepdims=True), axis=1, keepdims=True)
    factor = lax.rsqrt((total[1:2, 0:1] + gain_squares) / (DS * DT + DS) + epsilon)
    proj_out[...] = proj_out[...] * factor
    for k in range(4):
        gain_out[8 * k:8 * k + 8, :] = gain_grads[k] * factor
    loss_out[...] = total[2:3, :] / (32768 * DT)

    for copy in opened:
        copy.wait_send()


def finish(loss, hid, proj, gain, loss_out, hid_out, proj_out, gain_out, row, block, sem):
    parts = [pl.ds(i * 32, 32) for i in range(4)]
    loads = [pltpu.make_async_copy(hid.at[p], block.at[p], sem.at[i]) for i, p in enumerate(parts)]
    for copy in loads:
        copy.start()
    proj_out[...] = proj[...]
    loss_out[...] = loss[...]
    for i in range(32):
        row[:, i * PR:(i + 1) * PR] = gain[i:i + 1, :]
    for i in range(DS // 128):
        gain_out[i * 128:(i + 1) * 128] = row[0, i * 128:(i + 1) * 128]
    stores = []
    for i, p in enumerate(parts):
        loads[i].wait()
        stores.append(pltpu.make_async_copy(block.at[p], hid_out.at[p], sem.at[4 + i]))
        stores[i].start()
    for copy in stores:
        copy.wait()


def shards(student_hidden, norm_gain, projection, teacher_terms):
    teach = teacher_terms.reshape(4, 2, ROWS, DT)
    vmem = pl.BlockSpec(memory_space=pltpu.VMEM)
    V = pltpu.VMEM
    loss, hidden_grad, projection_update, gain_update = pl.pallas_call(
        kernel,
        out_shape=(
            jax.ShapeDtypeStruct((1, 128), F32),
            jax.ShapeDtypeStruct((ROWS, DS), BF16),
            jax.ShapeDtypeStruct((PR, PC), F32),
            jax.ShapeDtypeStruct((32, PR), F32),
        ),
        in_specs=[vmem, vmem, vmem, pl.BlockSpec(memory_space=pl.ANY)],
        out_specs=(vmem,) * 4,
        scratch_shapes=[
            V((4, ROWS, DS), BF16), V((DS, 4 * ROWS), BF16), V((4, 4, 2, PR, FX), BF16),
            V((4, ROWS, PC), BF16), V((4, ROWS, PC), BF16), V((2, 4, ROWS, PC), BF16),
            V((4, 4, ROWS, PC), BF16),
            V((4, 4, ROWS, PC), BF16),
            V((4, ROWS, PC), BF16), V((4, ROWS, PC), BF16),
            V((2, 4, ROWS, PC), BF16), V((2, 4, ROWS, PC), BF16), V((2, 4, ROWS, PC), BF16),
            V((4, ROWS, PC), BF16),
            V((2, ROWS, PC), BF16), V((2, ROWS, PC), BF16),
            V((4, ROWS, PC), BF16), V((4, ROWS, PC), BF16),
            V((4 * ROWS, FX), BF16), V((4 * ROWS, FX), BF16),
            V((2, 4, 4, 2, PR, PC), BF16), V((2, 4, 4, PR, PC), BF16),
            V((2, 2, PR, PC), BF16), V((2, 2, PR, PC), BF16),
            V((2, 4, PR, PC), BF16), V((2, 4, PR, PC), BF16), V((2, 4, PR, PC), BF16),
            V((2, 7, PR, HP), BF16), V((2, PR, HP), BF16),
            V((4, ROWS, DS), BF16), V((ROWS, HALF), BF16), V((ROWS, HALF), BF16),
            V((ROWS, DS), BF16), V((ROWS, DS), BF16),
            V((1, DS), F32), V((32, 128), F32), V((8, 128), F32), V((16, 128), F32),
            V((16, 8, 128), F32), V((16, 16, 128), F32),
            pltpu.SemaphoreType.DMA((N_MSG,)), pltpu.SemaphoreType.DMA((N_MSG,)),
            pltpu.SemaphoreType.DMA((24,)),
        ],
        compiler_params=pltpu.CompilerParams(
            collective_id=0, has_side_effects=True, vmem_limit_bytes=62 * 1024 * 1024
        ),
    )(student_hidden, norm_gain, projection, teach)
    loss, hidden_grad, projection_update, gain_update = pl.pallas_call(
        finish,
        out_shape=(
            jax.ShapeDtypeStruct((1, 128), F32),
            jax.ShapeDtypeStruct((ROWS, DS), BF16),
            jax.ShapeDtypeStruct((PR, PC), F32),
            jax.ShapeDtypeStruct((DS,), F32),
        ),
        in_specs=[vmem, pl.BlockSpec(memory_space=pl.ANY), vmem, vmem],
        out_specs=(vmem, pl.BlockSpec(memory_space=pl.ANY), vmem, vmem),
        scratch_shapes=[V((1, DS), F32), V((ROWS, DS), BF16), pltpu.SemaphoreType.DMA((8,))],
        compiler_params=pltpu.CompilerParams(vmem_limit_bytes=62 * 1024 * 1024),
    )(loss, hidden_grad, projection_update, gain_update)
    return loss[0, 0], hidden_grad, projection_update, gain_update


def solution(mesh):
    in_specs = (P(("dp", "tensor"), None), P(), P("dp", "tensor"), P("tensor", "dp", None))
    out_specs = (P(), P(("dp", "tensor"), None), P("dp", "tensor"), P())
    return jax.shard_map(shards, mesh=mesh, in_specs=in_specs, out_specs=out_specs, check_vma=False)
```
